32 devices in a mesh: dom: 8 (over z, core), help: 4 (over y, x).
Axes of the slice: x: 2, y: 2, z: 4, core: 2. Of those that a mesh axis runs over, the one named last changes fastest.
Arguments:
- positions: float32 [3, 8, 4, 3, 256], P(None, 'dom', 'help'), may hold values from 0 to 1
- velocities: float32 [3, 8, 4, 3, 256], P(None, 'dom', 'help'), may hold values from -6 to 6
- masses: float32 [8, 4, 3, 256], P('dom', 'help'), may hold values from 0.5 to 2
- counts: int32 [8, 4, 3], P('dom'), may hold values from 1 to 256, as said below
- neighbours: int32 [8, 4, 3, 27], P('dom'), may hold values from 0 to 2, as said below
Outputs:
- places: float32 [3, 8, 4, 3, 256], P(None, 'dom', 'help')
- speeds: float32 [3, 8, 4, 3, 256], P(None, 'dom', 'help')
The draws below stay inside these ranges and needn't reach their ends.
Inputs may be any that keep to these rules, and one draw needn't show every extreme that they name: `counts`: particles 0 to count - 1 of a bin are live; some bin holds 256. `neighbours`: each column of 3 bins is stored in its own order along y; entry k of bin (x, z, s) is the stored slot of the bin that lies at offset (k // 9 - 1, k % 3 - 1, k // 3 % 3 - 1) along (x, y, z) from it, periodically.
All inputs are finite; a program needn't handle non-finite values.
Results may differ from the reference program's by a relative error of at most 0.00016.
Values sent between devices are 32-bit elements; how exact they have to be, the bound alone decides.
A program may use at most 64 MiB of HBM per device.

```python
import math
import jax
import jax.numpy as jnp
from jax import lax

P_SIZE = 256
SLOTS = 27
GY = 3
SUBSTEPS = 3
GX = 8
GZ = 4


def pick_order(subkey):
    return jax.random.permutation(subkey, GY)


def column_orders(key):
    keys = jax.random.split(jax.random.fold_in(key, 11), GX * GZ)
    orders = jax.vmap(pick_order)(keys)
    return orders.reshape(GX, GZ, GY).astype(jnp.int32)


def draw_neighbours(key, part):
    orders = column_orders(key)
    inverse = jnp.argsort(orders, axis=-1, stable=True).astype(jnp.int32)
    columns = []
    for slot_index in range(SLOTS):
        along_x = slot_index // 9 - 1
        along_y = slot_index % 3 - 1
        along_z = slot_index // 3 % 3 - 1
        wanted = ((orders + along_y) % GY).astype(jnp.int32)
        moved = jnp.roll(inverse, (-along_x, -along_z), axis=(0, 1))
        columns.append(jnp.take_along_axis(moved, wanted, axis=2))
    return jnp.stack(columns, axis=-1).astype(jnp.int32)


def draw_counts(key, part):
    levels = jax.random.randint(jax.random.fold_in(key, 3), (GX, 1, 1), 1, 17).astype(jnp.int32)
    ceiling = jnp.maximum(levels * P_SIZE // 16, 1).astype(jnp.int32)
    base = jax.random.randint(key, (GX, GZ, GY), 1, P_SIZE + 1).astype(jnp.int32)
    base = (base - 1) % ceiling + 1
    flat = base.reshape(GX * GZ * GY)
    chosen_spot = jax.random.randint(jax.random.fold_in(key, 5), (), 0, GX * GZ * GY)
    filled = jnp.where(jnp.arange(GX * GZ * GY) == chosen_spot, P_SIZE, flat)
    return filled.reshape(GX, GZ, GY).astype(jnp.int32)


def block_levels(stream_key, extent, cuts, smallest, top_value):
    def one(axis_at, shards_of):
        heights = jax.random.uniform(jax.random.fold_in(jax.random.fold_in(stream_key, 6), axis_at), (shards_of,), jnp.float32, smallest / len(cuts), top_value / len(cuts))
        return jnp.repeat(jnp.exp(heights), extent[axis_at] // shards_of).reshape((-1,) + (1,) * (len(extent) - axis_at - 1))

    loudness = one(*cuts[0])
    for cut in cuts[1:]:
        loudness = loudness * one(*cut)
    return loudness


def scatter_about(own_key, shape, width, most, cuts=(), held_as=jnp.bfloat16):
    values = jax.random.normal(own_key, shape, jnp.float32) * width
    if len(cuts) > 0:
        values = block_levels(own_key, shape, cuts, -0.22, 0.18) * values
    return jnp.clip(values, min=-most, max=most).astype(held_as)


def setup_inputs(seed: int = 0) -> dict:
    key_of = jax.random.split(jax.random.key(seed), 6)
    positions = jnp.clip(1.0 * jax.random.uniform(key_of[0], (3, GX, GZ, GY, P_SIZE), jnp.float32) ** block_levels(key_of[0], (3, GX, GZ, GY, P_SIZE), ((1, 8), (2, 4)), -0.2, 0.2), 0.0, 1.0)
    velocities = scatter_about(key_of[1], (3, GX, GZ, GY, P_SIZE), 1.0, 6.0, ((1, 8), (2, 4)), jnp.float32)
    masses = jnp.clip(jnp.exp(math.log(2.0) - 1.3862944 * jax.random.uniform(key_of[2], (GX, GZ, GY, P_SIZE), jnp.float32) ** block_levels(key_of[2], (GX, GZ, GY, P_SIZE), ((0, 8), (1, 4)), -0.2, 0.2)), 0.5, 2.0)
    counts = draw_counts(jax.random.fold_in(key_of[5], 71), 0)
    neighbours = draw_neighbours(jax.random.fold_in(key_of[5], 71), 0)
    return {"positions": positions, "velocities": velocities, "masses": masses, "counts": counts, "neighbours": neighbours}


softening = 0.25
strength = 4.0
time_step = 0.2

def slot_offsets(slot_index):
    return (slot_index // 9 - 1, slot_index % 3 - 1, slot_index // 3 % 3 - 1)

def attract(targets, sources, offset):
    displaced = [sources[c][:, None, :] + offset[c] - targets[c][:, :, None] for c in range(3)]
    squared = displaced[0] * displaced[0] + displaced[1] * displaced[1] + displaced[2] * displaced[2] + softening
    inverse = lax.rsqrt(squared)
    weighting = sources[3][:, None, :] * inverse * inverse * inverse
    return jnp.stack([lax.optimization_barrier(jnp.sum(weighting * component, axis=2)) for component in displaced])

def reference(positions, velocities, masses, counts, neighbours):
    living = (jnp.arange(P_SIZE, dtype=jnp.int32)[None, None, None, :] < counts[..., None]).astype(jnp.float32)
    heavy = masses * living
    choose = (neighbours[..., None] == jnp.arange(GY, dtype=jnp.int32)[None, None, None, None, :]).astype(jnp.float32)
    places, speeds = (positions, velocities)
    for substep in range(SUBSTEPS):
        packet = jnp.concatenate([places, heavy[None]], axis=0)
        padded = jnp.concatenate([packet[:, -1:], packet, packet[:, :1]], axis=1)

        def forces_at(index):
            window = lax.dynamic_slice_in_dim(padded, index, 3, 1)
            targets = lax.dynamic_index_in_dim(places, index, 1, keepdims=False).reshape(3, GZ * GY, P_SIZE)
            picks = lax.dynamic_index_in_dim(choose, index, 0, keepdims=False)
            summed = jnp.zeros((3, GZ * GY, P_SIZE), jnp.float32)
            for slot_index in range(SLOTS):
                offset = slot_offsets(slot_index)
                column = jnp.roll(window[:, 1 + offset[0]], -offset[2], axis=1)
                chosen = jnp.einsum('czsp,zts->cztp', column, picks[:, :, slot_index, :], precision=lax.Precision.HIGHEST)
                summed = summed + attract(targets, chosen.reshape(4, GZ * GY, P_SIZE), (float(offset[0]), float(offset[1]), float(offset[2])))
            return summed.reshape(3, GZ, GY, P_SIZE)
        forces = lax.map(forces_at, jnp.arange(GX, dtype=jnp.int32))
        forces = jnp.moveaxis(forces, 0, 1)
        accel = forces * (strength / P_SIZE) * living[None]
        speeds = speeds + time_step * accel
        places = places + time_step * speeds
    return (places, speeds)
```

```python
import functools

import jax
import jax.numpy as jnp
from jax import lax
from jax.experimental import pallas as pl
from jax.experimental.pallas import tpu as pltpu
from jax.sharding import PartitionSpec as P

SUBSTEPS = 3
LANES = 128
GROUP = 32
TILES = 4

softening = 0.25
strength = 4.0
time_step = 0.2

SIDES = [(dx, dz) for dx in (-1, 0, 1) for dz in (-1, 0, 1)]
OWN = 4


def partner(dx, dz):
    def at(axis, step):
        count = lax.axis_size(axis)
        return lax.rem(lax.axis_index(axis) + (step + count), count)

    return {"dom": at("dom", dx), "help": at("help", dz)}


def greet():
    barrier = pltpu.get_barrier_semaphore()
    for index, (dx, dz) in enumerate(SIDES):
        if index != OWN:
            pl.semaphore_signal(
                barrier, inc=1, device_id=partner(dx, dz), device_id_type=pl.DeviceIdType.MESH
            )
    return barrier


def packet_copies(packet, halo, send_sem, recv_sem):
    copies = []
    for index, (dx, dz) in enumerate(SIDES):
        slot = len(SIDES) - 1 - index
        if index == OWN:
            copies.append(pltpu.make_async_copy(packet, halo.at[slot], send_sem.at[index]))
        else:
            copies.append(
                pltpu.make_async_remote_copy(
                    src_ref=packet,
                    dst_ref=halo.at[slot],
                    send_sem=send_sem.at[index],
                    recv_sem=recv_sem.at[slot],
                    device_id=partner(dx, dz),
                    device_id_type=pl.DeviceIdType.MESH,
                )
            )
    return copies


def first_exchange(positions, masses, counts, halo, all_counts, packet, send_sem, recv_sem, count_send, count_recv):
    barrier = greet()
    bins = positions.shape[3]
    packet[...] = jnp.zeros_like(packet)
    for s in range(bins):
        for c in range(3):
            packet[4 * s + c : 4 * s + c + 1, :] = positions[c, 0, 0, s : s + 1, :]
        packet[4 * s + 3 : 4 * s + 4, :] = masses[0, 0, s : s + 1, :]
    pl.semaphore_wait(barrier, len(SIDES) - 1)
    copies = packet_copies(packet, halo, send_sem, recv_sem)
    for dx in (-1, 0, 1):
        place = all_counts.at[pl.ds(1 - dx, 1)]
        if dx == 0:
            copies.append(pltpu.make_async_copy(counts, place, count_send.at[1]))
        else:
            copies.append(
                pltpu.make_async_remote_copy(
                    src_ref=counts,
                    dst_ref=place,
                    send_sem=count_send.at[1 + dx],
                    recv_sem=count_recv.at[1 - dx],
                    device_id=partner(dx, 0),
                    device_id_type=pl.DeviceIdType.MESH,
                )
            )
    for copy in copies:
        copy.start()
    for copy in copies:
        copy.wait()


def later_exchange(packet, halo, send_sem, recv_sem):
    barrier = greet()
    pl.semaphore_wait(barrier, len(SIDES) - 1)
    copies = packet_copies(packet, halo, send_sem, recv_sem)
    for copy in copies:
        copy.start()
    for copy in copies:
        copy.wait()


def step_kernel(last, all_counts, links, halo, speeds, *rest):
    if last:
        places_out, speeds_out, sources, spread, totals = rest
    else:
        packet_out, speeds_out, sources, spread, totals = rest
    helpers = all_counts.shape[1]
    bins = all_counts.shape[2]
    slots = halo.shape[2]
    halves = slots // LANES
    z = lax.axis_index("help")
    lane = lax.broadcasted_iota(jnp.int32, (8, LANES), 1)
    row = lax.broadcasted_iota(jnp.int32, (8, LANES), 0)

    sources[0] = jnp.zeros((8, LANES), jnp.float32)
    filled = jnp.int32(0)
    for index, (dx, dz) in enumerate(SIDES):
        column_z = lax.rem(z + (dz + helpers), helpers)
        for s in range(bins):
            live = all_counts[1 + dx, column_z, s]
            shift = jnp.where(row == 0, float(dx), jnp.where(row == bins + 1, float(dz), 0.0))
            for t in range(bins):
                below = links[0, z, t, (dx + 1) * 9 + (dz + 1) * 3] == s
                above = links[0, z, t, (dx + 1) * 9 + (dz + 1) * 3 + 2] == s
                along = jnp.where(below, -1.0, jnp.where(above, 1.0, 0.0)).astype(jnp.float32)
                shift = jnp.where(row == 1 + t, along, shift)
            tile = filled // LANES
            turn = lax.rem(filled, LANES)
            kept = lane >= turn
            carried = sources[tile]
            for half in range(halves):
                part = halo[index, 4 * s : 4 * s + 4, half * LANES : (half + 1) * LANES]
                block = jnp.concatenate(
                    [part[0:1]] + [part[1:2]] * bins + [part[2:3], part[3:4]]
                    + [part[3:4]] * (8 - bins - 3),
                    axis=0,
                )
                block = jnp.where(lane + half * LANES < live, block + shift, 0.0)
                turned = pltpu.roll(block, turn, 1)
                sources[tile + half] = carried + jnp.where(kept, turned, 0.0)
                carried = jnp.where(kept, 0.0, turned)
            sources[tile + halves] = carried
            filled = filled + live
    used = (filled + LANES - 1) // LANES
    for extra in range(TILES):
        sources[used + extra] = jnp.zeros((8, LANES), jnp.float32)
    rounds = (used + TILES - 1) // TILES

    for t in range(bins):
        live = all_counts[1, z, t]

        for half in range(halves):

            @pl.when(live > half * LANES)
            def _():
                for c in range(3):
                    line = halo[OWN, 4 * t + c : 4 * t + c + 1, half * LANES : (half + 1) * LANES]
                    spread[c, half * LANES : (half + 1) * LANES, :] = jnp.transpose(
                        jnp.broadcast_to(line, (LANES, LANES))
                    )

        def work(group, carry):
            rows = pl.ds(pl.multiple_of(group * GROUP, GROUP), GROUP)
            targets = [spread[c, rows, :] for c in range(3)]

            def add(step, sums):
                sums = list(sums)
                for k in range(TILES):
                    tile = step * TILES + k
                    sx = sources[tile, 0:1, :]
                    sy = sources[tile, 1 + t : 2 + t, :]
                    sz = sources[tile, bins + 1 : bins + 2, :]
                    mass = sources[tile, bins + 2 : bins + 3, :]
                    ex = sx - targets[0]
                    ey = sy - targets[1]
                    ez = sz - targets[2]
                    inverse = lax.rsqrt(ex * ex + ey * ey + (ez * ez + softening))
                    weight = (mass * inverse) * (inverse * inverse)
                    sums[0] = sums[0] + weight * ex
                    sums[1] = sums[1] + weight * ey
                    sums[2] = sums[2] + weight * ez
                return tuple(sums)

            zero = jnp.zeros((GROUP, LANES), jnp.float32)
            sums = lax.fori_loop(0, rounds, add, (zero, zero, zero))
            for c in range(3):
                totals[c, rows, :] = sums[c]
            return carry

        lax.fori_loop(0, (live + GROUP - 1) // GROUP, work, 0)

        for half in range(halves):
            lanes = slice(half * LANES, (half + 1) * LANES)
            alive = lane[0:1] + half * LANES < live
            for c in range(3):
                summed = jnp.sum(jnp.transpose(totals[c, lanes, :]), axis=0, keepdims=True)
                accel = jnp.where(alive, summed * (strength / slots), 0.0)
                speed = speeds[c, 0, 0, t : t + 1, lanes] + time_step * accel
                place = halo[OWN, 4 * t + c : 4 * t + c + 1, lanes] + time_step * speed
                speeds_out[c, 0, 0, t : t + 1, lanes] = speed
                if last:
                    places_out[c, 0, 0, t : t + 1, lanes] = place
                else:
                    packet_out[4 * t + c : 4 * t + c + 1, lanes] = place
        if not last:
            packet_out[4 * t + 3 : 4 * t + 4, :] = halo[OWN, 4 * t + 3 : 4 * t + 4, :]
    if not last:
        used_rows = 4 * bins
        if packet_out.shape[0] > used_rows:
            packet_out[used_rows:, :] = jnp.zeros(
                (packet_out.shape[0] - used_rows, slots), jnp.float32
            )


def on_device(positions, velocities, masses, counts, neighbours):
    bins, slots = positions.shape[3:]
    helpers = counts.shape[1]
    rows = (4 * bins + 7) // 8 * 8
    vmem = pl.BlockSpec(memory_space=pltpu.VMEM)
    smem = pl.BlockSpec(memory_space=pltpu.SMEM)
    anywhere = pl.BlockSpec(memory_space=pl.ANY)
    dma = pltpu.SemaphoreType.DMA
    halo_shape = jax.ShapeDtypeStruct((len(SIDES), rows, slots), jnp.float32)
    packet_shape = jax.ShapeDtypeStruct((rows, slots), jnp.float32)
    state_shape = jax.ShapeDtypeStruct(positions.shape, jnp.float32)

    halo, all_counts = pl.pallas_call(
        first_exchange,
        out_shape=(halo_shape, jax.ShapeDtypeStruct((3, helpers, bins), jnp.int32)),
        in_specs=[vmem, vmem, anywhere],
        out_specs=(anywhere, anywhere),
        scratch_shapes=[
            pltpu.VMEM((rows, slots), jnp.float32),
            dma((9,)),
            dma((9,)),
            dma((3,)),
            dma((3,)),
        ],
        compiler_params=pltpu.CompilerParams(collective_id=0, has_side_effects=True),
        name="first_exchange",
    )(positions, masses, counts)

    exchange = pl.pallas_call(
        later_exchange,
        out_shape=halo_shape,
        in_specs=[anywhere],
        out_specs=anywhere,
        scratch_shapes=[dma((9,)), dma((9,))],
        compiler_params=pltpu.CompilerParams(collective_id=1, has_side_effects=True),
        name="later_exchange",
    )

    tiles = len(SIDES) * bins * slots // LANES + slots // LANES + 1 + TILES
    speeds = velocities
    for substep in range(SUBSTEPS):
        last = substep == SUBSTEPS - 1
        state, speeds = pl.pallas_call(
            functools.partial(step_kernel, last),
            out_shape=(state_shape if last else packet_shape, state_shape),
            in_specs=[smem, smem, vmem, vmem],
            out_specs=(vmem, vmem),
            scratch_shapes=[
                pltpu.VMEM((tiles, 8, LANES), jnp.float32),
                pltpu.VMEM((3, slots, LANES), jnp.float32),
                pltpu.VMEM((3, slots, LANES), jnp.float32),
            ],
            compiler_params=pltpu.CompilerParams(vmem_limit_bytes=32 * 1024 * 1024),
            name="step_last" if last else "step",
        )(all_counts, neighbours, halo, speeds)
        if not last:
            halo = exchange(state)
    return state, speeds


def solution(mesh):
    return jax.shard_map(
        on_device,
        mesh=mesh,
        in_specs=(
            P(None, "dom", "help", None, None),
            P(None, "dom", "help", None, None),
            P("dom", "help", None, None),
            P("dom", None, None),
            P("dom", None, None, None),
        ),
        out_specs=(P(None, "dom", "help", None, None), P(None, "dom", "help", None, None)),
        check_vma=False,
    )
```

```python
import jax
import jax.numpy as jnp
from jax import lax
from jax.experimental import pallas as pl
from jax.experimental.pallas import tpu as pltpu
from jax.sharding import PartitionSpec as P

SUBSTEPS = 3
LANES = 128
GROUP = 32
TILES = 4

softening = 0.25
strength = 4.0
time_step = 0.2

SIDES = [(dx, dz) for dx in (-1, 0, 1) for dz in (-1, 0, 1) if (dx, dz) != (0, 0)]


def partner(dx, dz):
    def at(axis, step):
        count = lax.axis_size(axis)
        return lax.rem(lax.axis_index(axis) + (step + count), count)

    return {"dom": at("dom", dx), "help": at("help", dz)}


def greet():
    barrier = pltpu.get_barrier_semaphore()
    for dx, dz in SIDES:
        pl.semaphore_signal(
            barrier, inc=1, device_id=partner(dx, dz), device_id_type=pl.DeviceIdType.MESH
        )
    pl.semaphore_wait(barrier, len(SIDES))


def column_copies(column, halo, send_sem, recv_sem):
    last = len(SIDES) - 1
    return [
        pltpu.make_async_remote_copy(
            src_ref=column,
            dst_ref=halo.at[last - index],
            send_sem=send_sem.at[index],
            recv_sem=recv_sem.at[last - index],
            device_id=partner(dx, dz),
            device_id_type=pl.DeviceIdType.MESH,
        )
        for index, (dx, dz) in enumerate(SIDES)
    ]


def first_exchange(places, masses, counts, halo, mass_halo, all_counts, *sems):
    greet()
    copies = column_copies(places, halo, sems[0], sems[1])
    copies += column_copies(masses, mass_halo, sems[2], sems[3])
    for dx in (-1, 1):
        copies.append(
            pltpu.make_async_remote_copy(
                src_ref=counts,
                dst_ref=all_counts.at[1 - dx],
                send_sem=sems[4].at[1 + dx],
                recv_sem=sems[5].at[1 - dx],
                device_id=partner(dx, 0),
                device_id_type=pl.DeviceIdType.MESH,
            )
        )
    for copy in copies:
        copy.start()
    all_counts[1] = counts[...]
    for copy in copies:
        copy.wait()


def later_exchange(places, halo, send_sem, recv_sem):
    greet()
    copies = column_copies(places, halo, send_sem, recv_sem)
    for copy in copies:
        copy.start()
    for copy in copies:
        copy.wait()


def step_kernel(all_counts, links, halo, mass_halo, places, masses, speeds, places_out, speeds_out, sources, spread, totals):
    bins = masses.shape[0]
    helpers = all_counts.shape[3]
    slots = masses.shape[2]
    halves = slots // LANES
    z = lax.axis_index("help")
    lane = lax.broadcasted_iota(jnp.int32, (8, LANES), 1)
    row = lax.broadcasted_iota(jnp.int32, (8, LANES), 0)

    sources[0] = jnp.zeros((8, LANES), jnp.float32)
    filled = jnp.int32(0)
    for dx in (-1, 0, 1):
        for dz in (-1, 0, 1):
            column_z = lax.rem(z + (dz + helpers), helpers)
            if (dx, dz) == (0, 0):
                column, weights = places, masses
            else:
                column, weights = (ref.at[SIDES.index((dx, dz))] for ref in (halo, mass_halo))
            for s in range(bins):
                live = all_counts[1 + dx, s, 0, column_z]
                shift = jnp.where(row == 0, float(dx), jnp.where(row == bins + 1, float(dz), 0.0))
                for t in range(bins):
                    below = links[0, t, z, (dx + 1) * 9 + (dz + 1) * 3] == s
                    above = links[0, t, z, (dx + 1) * 9 + (dz + 1) * 3 + 2] == s
                    along = jnp.where(below, -1.0, jnp.where(above, 1.0, 0.0)).astype(jnp.float32)
                    shift = jnp.where(row == 1 + t, along, shift)
                tile = filled // LANES
                turn = lax.rem(filled, LANES)
                kept = lane >= turn
                carried = sources[tile]
                for half in range(halves):
                    lanes = slice(half * LANES, (half + 1) * LANES)
                    line = [
                        jnp.broadcast_to(part, (8, LANES))
                        for part in [column[c * bins + s, :, lanes] for c in range(3)]
                        + [weights[s, :, lanes]]
                    ]
                    block = jnp.where(row == bins + 1, line[2], line[3])
                    block = jnp.where(row <= bins, line[1], block)
                    block = jnp.where(row == 0, line[0], block)
                    block = jnp.where(lane + half * LANES < live, block + shift, 0.0)
                    turned = pltpu.roll(block, turn, 1)
                    sources[tile + half] = carried + jnp.where(kept, turned, 0.0)
                    carried = jnp.where(kept, 0.0, turned)
                sources[tile + halves] = carried
                filled = filled + live
    used = (filled + LANES - 1) // LANES
    for extra in range(TILES):
        sources[used + extra] = jnp.zeros((8, LANES), jnp.float32)
    rounds = (used + TILES - 1) // TILES

    for t in range(bins):
        live = all_counts[1, t, 0, z]

        for half in range(halves):

            @pl.when(live > half * LANES)
            def _():
                for c in range(3):
                    line = places[c * bins + t, :, half * LANES : (half + 1) * LANES]
                    spread[c, half * LANES : (half + 1) * LANES, :] = jnp.transpose(
                        jnp.broadcast_to(line, (LANES, LANES))
                    )

        def work(group, carry):
            rows = pl.ds(pl.multiple_of(group * GROUP, GROUP), GROUP)
            targets = [spread[c, rows, :] for c in range(3)]

            def add(step, sums):
                sums = list(sums)
                for k in range(TILES):
                    tile = step * TILES + k
                    sx = sources[tile, 0:1, :]
                    sy = sources[tile, 1 + t : 2 + t, :]
                    sz = sources[tile, bins + 1 : bins + 2, :]
                    mass = sources[tile, bins + 2 : bins + 3, :]
                    ex = sx - targets[0]
                    ey = sy - targets[1]
                    ez = sz - targets[2]
                    inverse = lax.rsqrt(ex * ex + ey * ey + (ez * ez + softening))
                    weight = (mass * inverse) * (inverse * inverse)
                    sums[0] = sums[0] + weight * ex
                    sums[1] = sums[1] + weight * ey
                    sums[2] = sums[2] + weight * ez
                return tuple(sums)

            zero = jnp.zeros((GROUP, LANES), jnp.float32)
            sums = lax.fori_loop(0, rounds, add, (zero, zero, zero))
            for c in range(3):
                totals[c, rows, :] = sums[c]
            return carry

        lax.fori_loop(0, (live + GROUP - 1) // GROUP, work, 0)

        for half in range(halves):
            lanes = slice(half * LANES, (half + 1) * LANES)
            alive = lane[0:1] + half * LANES < live
            for c in range(3):
                at = c * bins + t
                summed = jnp.sum(jnp.transpose(totals[c, lanes, :]), axis=0, keepdims=True)
                accel = jnp.where(alive, summed * (strength / slots), 0.0)
                speed = speeds[at, :, lanes] + time_step * accel
                speeds_out[at, :, lanes] = speed
                places_out[at, :, lanes] = places[at, :, lanes] + time_step * speed


def on_device(positions, velocities, masses, counts, neighbours):
    bins, slots = positions.shape[3:]
    helpers = counts.shape[1]
    sides = len(SIDES)
    vmem = pl.BlockSpec(memory_space=pltpu.VMEM)
    smem = pl.BlockSpec(memory_space=pltpu.SMEM)
    dma = pltpu.SemaphoreType.DMA

    def floats(*shape):
        return jax.ShapeDtypeStruct(shape, jnp.float32)

    places = positions.reshape(3 * bins, 1, slots)
    speeds = velocities.reshape(3 * bins, 1, slots)
    masses = masses.reshape(bins, 1, slots)
    counts = counts.transpose(2, 0, 1)
    links = neighbours.transpose(0, 2, 1, 3)

    halo, mass_halo, all_counts = pl.pallas_call(
        first_exchange,
        out_shape=(
            floats(sides, 3 * bins, 1, slots),
            floats(sides, bins, 1, slots),
            jax.ShapeDtypeStruct((3, bins, 1, helpers), jnp.int32),
        ),
        in_specs=[vmem] * 3,
        out_specs=(vmem,) * 3,
        scratch_shapes=[dma((sides,))] * 4 + [dma((3,))] * 2,
        compiler_params=pltpu.CompilerParams(collective_id=0, has_side_effects=True),
        name="first_exchange",
    )(places, masses, counts)

    exchange = pl.pallas_call(
        later_exchange,
        out_shape=floats(sides, 3 * bins, 1, slots),
        in_specs=[vmem],
        out_specs=vmem,
        scratch_shapes=[dma((sides,))] * 2,
        compiler_params=pltpu.CompilerParams(collective_id=1, has_side_effects=True),
        name="later_exchange",
    )

    tiles = (sides + 1) * bins * slots // LANES + slots // LANES + 1 + TILES
    step = pl.pallas_call(
        step_kernel,
        out_shape=(floats(3 * bins, 1, slots),) * 2,
        in_specs=[smem] * 2 + [vmem] * 5,
        out_specs=(vmem,) * 2,
        scratch_shapes=[
            pltpu.VMEM((tiles, 8, LANES), jnp.float32),
            pltpu.VMEM((3, slots, LANES), jnp.float32),
            pltpu.VMEM((3, slots, LANES), jnp.float32),
        ],
        compiler_params=pltpu.CompilerParams(vmem_limit_bytes=32 * 1024 * 1024),
        name="step",
    )
    for substep in range(SUBSTEPS):
        if substep > 0:
            halo = exchange(places)
        places, speeds = step(all_counts, links, halo, mass_halo, places, masses, speeds)
    return places.reshape(positions.shape), speeds.reshape(velocities.shape)


def solution(mesh):
    return jax.shard_map(
        on_device,
        mesh=mesh,
        in_specs=(
            P(None, "dom", "help", None, None),
            P(None, "dom", "help", None, None),
            P("dom", "help", None, None),
            P("dom", None, None),
            P("dom", None, None, None),
        ),
        out_specs=(P(None, "dom", "help", None, None), P(None, "dom", "help", None, None)),
        check_vma=False,
    )
```

```python
import functools

import jax
import jax.numpy as jnp
from jax import lax
from jax.experimental import pallas as pl
from jax.experimental.pallas import tpu as pltpu
from jax.sharding import PartitionSpec as P

SUBSTEPS = 3
LANES = 128
GROUP = 32
TILES = 4

softening = 0.25
strength = 4.0
time_step = 0.2

SIDES = [(dx, dz) for dx in (-1, 0, 1) for dz in (-1, 0, 1) if (dx, dz) != (0, 0)]


def partner(dx, dz):
    def at(axis, step):
        count = lax.axis_size(axis)
        return lax.rem(lax.axis_index(axis) + (step + count), count)

    return {"dom": at("dom", dx), "help": at("help", dz)}


def greet():
    barrier = pltpu.get_barrier_semaphore()
    for dx, dz in SIDES:
        pl.semaphore_signal(
            barrier, inc=1, device_id=partner(dx, dz), device_id_type=pl.DeviceIdType.MESH
        )
    pl.semaphore_wait(barrier, len(SIDES))


def column_copies(column, halo, send_sem, recv_sem):
    last = len(SIDES) - 1
    return [
        pltpu.make_async_remote_copy(
            src_ref=column,
            dst_ref=halo.at[last - index],
            send_sem=send_sem.at[index],
            recv_sem=recv_sem.at[last - index],
            device_id=partner(dx, dz),
            device_id_type=pl.DeviceIdType.MESH,
        )
        for index, (dx, dz) in enumerate(SIDES)
    ]


def first_exchange(places, masses, counts, halo, mass_halo, all_counts, *sems):
    greet()
    copies = column_copies(places, halo, sems[0], sems[1])
    copies += column_copies(masses, mass_halo, sems[2], sems[3])
    for dx in (-1, 1):
        copies.append(
            pltpu.make_async_remote_copy(
                src_ref=counts,
                dst_ref=all_counts.at[1 - dx],
                send_sem=sems[4].at[1 + dx],
                recv_sem=sems[5].at[1 - dx],
                device_id=partner(dx, 0),
                device_id_type=pl.DeviceIdType.MESH,
            )
        )
    copies.append(pltpu.make_async_copy(counts, all_counts.at[1], sems[4].at[1]))
    for copy in copies:
        copy.start()
    for copy in copies:
        copy.wait()


def later_exchange(places, halo, send_sem, recv_sem):
    greet()
    copies = column_copies(places, halo, send_sem, recv_sem)
    for copy in copies:
        copy.start()
    for copy in copies:
        copy.wait()


def step_kernel(
    last, counts_hbm, links_hbm, halo_hbm, mass_halo_hbm, places, masses, speeds,
    places_hbm, speeds_out, all_counts, links, halo, mass_halo, places_out, speeds_now,
    sources, spread, totals, columns, sems,
):
    fetches = [
        pltpu.make_async_copy(there, here, sems.at[i])
        for i, (there, here) in enumerate(
            [(counts_hbm, all_counts), (links_hbm, links), (halo_hbm, halo), (mass_halo_hbm, mass_halo)]
        )
    ]
    for fetch in fetches:
        fetch.start()
    bins = masses.shape[0]
    helpers = all_counts.shape[3]
    slots = masses.shape[2]
    halves = slots // LANES
    z = lax.axis_index("help")
    lane = lax.broadcasted_iota(jnp.int32, (8, LANES), 1)
    row = lax.broadcasted_iota(jnp.int32, (8, LANES), 0)
    wide_lane = lax.broadcasted_iota(jnp.int32, (LANES, LANES), 1)

    columns[...] = jnp.zeros_like(columns)
    for half in range(halves):
        lanes = slice(half * LANES, (half + 1) * LANES)
        for i in range(3 * bins):
            columns[i : i + 1, :] = places[i, :, lanes]
        turned = jnp.transpose(columns[...])
        for i in range(3 * bins):
            spread[i, lanes, :] = jnp.broadcast_to(turned[:, i : i + 1], (LANES, LANES))
    for fetch in fetches:
        fetch.wait()

    sources[0] = jnp.zeros((8, LANES), jnp.float32)
    filled = jnp.int32(0)
    for dx in (-1, 0, 1):
        for dz in (-1, 0, 1):
            column_z = lax.rem(z + (dz + helpers), helpers)
            if (dx, dz) == (0, 0):
                column, weights = places, masses
            else:
                column, weights = (ref.at[SIDES.index((dx, dz))] for ref in (halo, mass_halo))
            for s in range(bins):
                live = all_counts[1 + dx, s, 0, column_z]
                shift = jnp.where(row == 0, float(dx), jnp.where(row == bins + 1, float(dz), 0.0))
                for t in range(bins):
                    below = links[0, t, z, (dx + 1) * 9 + (dz + 1) * 3] == s
                    above = links[0, t, z, (dx + 1) * 9 + (dz + 1) * 3 + 2] == s
                    along = jnp.where(below, -1.0, jnp.where(above, 1.0, 0.0)).astype(jnp.float32)
                    shift = jnp.where(row == 1 + t, along, shift)
                tile = filled // LANES
                turn = lax.rem(filled, LANES)
                kept = lane >= turn
                carried = sources[tile]
                for half in range(halves):
                    lanes = slice(half * LANES, (half + 1) * LANES)
                    line = [
                        jnp.broadcast_to(part, (8, LANES))
                        for part in [column[c * bins + s, :, lanes] for c in range(3)]
                        + [weights[s, :, lanes]]
                    ]
                    block = jnp.where(row == bins + 1, line[2], line[3])
                    block = jnp.where(row <= bins, line[1], block)
                    block = jnp.where(row == 0, line[0], block)
                    block = jnp.where(lane + half * LANES < live, block + shift, 0.0)
                    turned = pltpu.roll(block, turn, 1)
                    sources[tile + half] = carried + jnp.where(kept, turned, 0.0)
                    carried = jnp.where(kept, 0.0, turned)
                sources[tile + halves] = carried
                filled = filled + live
    used = (filled + LANES - 1) // LANES
    for extra in range(TILES):
        sources[used + extra] = jnp.zeros((8, LANES), jnp.float32)
    rounds = (used + TILES - 1) // TILES

    for t in range(bins):
        live = all_counts[1, t, 0, z]

        def work(group, carry):
            rows = pl.ds(pl.multiple_of(group * GROUP, GROUP), GROUP)
            targets = [spread[c * bins + t, rows, :] for c in range(3)]

            def add(step, sums):
                sums = list(sums)
                for k in range(TILES):
                    tile = step * TILES + k
                    sx = sources[tile, 0:1, :]
                    sy = sources[tile, 1 + t : 2 + t, :]
                    sz = sources[tile, bins + 1 : bins + 2, :]
                    mass = sources[tile, bins + 2 : bins + 3, :]
                    ex = sx - targets[0]
                    ey = sy - targets[1]
                    ez = sz - targets[2]
                    inverse = lax.rsqrt(ex * ex + ey * ey + (ez * ez + softening))
                    weight = (mass * inverse) * (inverse * inverse)
                    sums[0] = sums[0] + weight * ex
                    sums[1] = sums[1] + weight * ey
                    sums[2] = sums[2] + weight * ez
                return tuple(sums)

            zero = jnp.zeros((GROUP, LANES), jnp.float32)
            sums = lax.fori_loop(0, rounds, add, (zero, zero, zero))
            for c in range(3):
                totals[c * bins + t, rows, :] = sums[c]
            return carry

        lax.fori_loop(0, (live + GROUP - 1) // GROUP, work, 0)

    speeds_next = speeds_now if last else speeds_out
    for half in range(halves):
        lanes = slice(half * LANES, (half + 1) * LANES)
        columns[...] = jnp.zeros_like(columns)
        for t in range(bins):

            @pl.when(all_counts[1, t, 0, z] > half * LANES)
            def _():
                found = columns[...]
                for c in range(3):
                    at = c * bins + t
                    found = jnp.where(
                        wide_lane == at, jnp.sum(totals[at, lanes, :], axis=1, keepdims=True), found
                    )
                columns[...] = found

        summed = jnp.transpose(columns[...])
        for t in range(bins):
            alive = lane[0:1] + half * LANES < all_counts[1, t, 0, z]
            for c in range(3):
                at = c * bins + t
                accel = jnp.where(alive, summed[at : at + 1] * (strength / slots), 0.0)
                speed = speeds[at, :, lanes] + time_step * accel
                speeds_next[at, :, lanes] = speed
                places_out[at, :, lanes] = places[at, :, lanes] + time_step * speed
    stores = [pltpu.make_async_copy(places_out, places_hbm, sems.at[0])]
    if last:
        stores.append(pltpu.make_async_copy(speeds_now, speeds_out, sems.at[1]))
    for store in stores:
        store.start()
    for store in stores:
        store.wait()


def on_device(positions, velocities, masses, counts, neighbours):
    bins, slots = positions.shape[3:]
    helpers = counts.shape[1]
    sides = len(SIDES)
    vmem = pl.BlockSpec(memory_space=pltpu.VMEM)
    hbm = pl.BlockSpec(memory_space=pltpu.HBM)
    dma = pltpu.SemaphoreType.DMA

    def floats(*shape):
        return jax.ShapeDtypeStruct(shape, jnp.float32)

    places = positions.reshape(3 * bins, 1, slots)
    speeds = velocities.reshape(3 * bins, 1, slots)
    masses = masses.reshape(bins, 1, slots)
    counts = counts.transpose(2, 0, 1)
    links = neighbours.transpose(0, 2, 1, 3)

    halo, mass_halo, all_counts = pl.pallas_call(
        first_exchange,
        out_shape=(
            floats(sides, 3 * bins, 1, slots),
            floats(sides, bins, 1, slots),
            jax.ShapeDtypeStruct((3, bins, 1, helpers), jnp.int32),
        ),
        in_specs=[hbm] * 3,
        out_specs=(hbm,) * 3,
        scratch_shapes=[dma((sides,))] * 4 + [dma((3,))] * 2,
        compiler_params=pltpu.CompilerParams(collective_id=0, has_side_effects=True),
        name="first_exchange",
    )(places, masses, counts)

    exchange = pl.pallas_call(
        later_exchange,
        out_shape=floats(sides, 3 * bins, 1, slots),
        in_specs=[hbm],
        out_specs=hbm,
        scratch_shapes=[dma((sides,))] * 2,
        compiler_params=pltpu.CompilerParams(collective_id=1, has_side_effects=True),
        name="later_exchange",
    )

    tiles = (sides + 1) * bins * slots // LANES + slots // LANES + 1 + TILES
    state = floats(3 * bins, 1, slots)

    def step(last, *operands):
        return pl.pallas_call(
            functools.partial(step_kernel, last),
            out_shape=(state, state),
            in_specs=[hbm] * 4 + [vmem] * 3,
            out_specs=(hbm, hbm if last else vmem),
            scratch_shapes=[
                pltpu.SMEM((3, bins, 1, helpers), jnp.int32),
                pltpu.SMEM(links.shape, jnp.int32),
                pltpu.VMEM(halo.shape, jnp.float32),
                pltpu.VMEM(mass_halo.shape, jnp.float32),
                pltpu.VMEM(state.shape, jnp.float32),
                pltpu.VMEM(state.shape, jnp.float32),
                pltpu.VMEM((tiles, 8, LANES), jnp.float32),
                pltpu.VMEM((3 * bins, slots, LANES), jnp.float32),
                pltpu.VMEM((3 * bins, slots, LANES), jnp.float32),
                pltpu.VMEM((LANES, LANES), jnp.float32),
                dma((4,)),
            ],
            compiler_params=pltpu.CompilerParams(vmem_limit_bytes=32 * 1024 * 1024),
            name="step",
        )(*operands)

    for substep in range(SUBSTEPS):
        if substep > 0:
            halo = exchange(places)
        places, speeds = step(
            substep == SUBSTEPS - 1, all_counts, links, halo, mass_halo, places, masses, speeds
        )
    return places.reshape(positions.shape), speeds.reshape(velocities.shape)


def solution(mesh):
    return jax.shard_map(
        on_device,
        mesh=mesh,
        in_specs=(
            P(None, "dom", "help", None, None),
            P(None, "dom", "help", None, None),
            P("dom", "help", None, None),
            P("dom", None, None),
            P("dom", None, None, None),
        ),
        out_specs=(P(None, "dom", "help", None, None), P(None, "dom", "help", None, None)),
        check_vma=False,
    )
```

```python
import jax
import jax.numpy as jnp
from jax import lax
from jax.experimental import pallas as pl
from jax.experimental.pallas import tpu as pltpu
from jax.sharding import PartitionSpec as P

SUBSTEPS = 3
LANES = 128
GROUP = 32
TILES = (16, 8, 4, 2, 1)

softening = 0.25
strength = 4.0
time_step = 0.2

SIDES = [(dx, dz) for dx in (-1, 0, 1) for dz in (-1, 0, 1) if (dx, dz) != (0, 0)]


def partner(dx, dz):
    def at(axis, step):
        count = lax.axis_size(axis)
        return lax.rem(lax.axis_index(axis) + (step + count), count)

    return {"dom": at("dom", dx), "help": at("help", dz)}


def greet():
    barrier = pltpu.get_barrier_semaphore()
    for dx, dz in SIDES:
        pl.semaphore_signal(
            barrier, inc=1, device_id=partner(dx, dz), device_id_type=pl.DeviceIdType.MESH
        )
    pl.semaphore_wait(barrier, len(SIDES))


def column_copies(column, halo, send_sem, recv_sem):
    last = len(SIDES) - 1
    return [
        pltpu.make_async_remote_copy(
            src_ref=column,
            dst_ref=halo.at[last - index],
            send_sem=send_sem.at[index],
            recv_sem=recv_sem.at[last - index],
            device_id=partner(dx, dz),
            device_id_type=pl.DeviceIdType.MESH,
        )
        for index, (dx, dz) in enumerate(SIDES)
    ]


def first_exchange(places, masses, counts, halo, mass_halo, all_counts, *sems):
    greet()
    copies = column_copies(places, halo, sems[0], sems[1])
    copies += column_copies(masses, mass_halo, sems[2], sems[3])
    for dx in (-1, 1):
        copies.append(
            pltpu.make_async_remote_copy(
                src_ref=counts,
                dst_ref=all_counts.at[1 - dx],
                send_sem=sems[4].at[1 + dx],
                recv_sem=sems[5].at[1 - dx],
                device_id=partner(dx, 0),
                device_id_type=pl.DeviceIdType.MESH,
            )
        )
    copies.append(pltpu.make_async_copy(counts, all_counts.at[1], sems[4].at[1]))
    for copy in copies:
        copy.start()
    for copy in copies:
        copy.wait()


def later_exchange(places, halo, send_sem, recv_sem):
    greet()
    copies = column_copies(places, halo, send_sem, recv_sem)
    for copy in copies:
        copy.start()
    for copy in copies:
        copy.wait()


def step_kernel(
    counts_in, links_in, halo_in, mass_halo_in, places_in, masses_in, speeds_in,
    places_out, speeds_out, all_counts, links, halo, mass_halo, places, masses, speeds,
    sources, spread, totals, columns, sems,
):
    pairs = [
        (places_in, places),
        (counts_in, all_counts),
        (links_in, links),
        (halo_in, halo),
        (mass_halo_in, mass_halo),
        (masses_in, masses),
        (speeds_in, speeds),
    ]
    fetches = [
        pltpu.make_async_copy(there, here, sems.at[i]) for i, (there, here) in enumerate(pairs)
    ]
    for fetch in fetches:
        fetch.start()
    bins = masses.shape[0]
    helpers = all_counts.shape[3]
    slots = masses.shape[2]
    halves = slots // LANES
    z = lax.axis_index("help")
    lane = lax.broadcasted_iota(jnp.int32, (8, LANES), 1)
    row = lax.broadcasted_iota(jnp.int32, (8, LANES), 0)
    wide_lane = lax.broadcasted_iota(jnp.int32, (LANES, LANES), 1)

    columns[...] = jnp.zeros_like(columns)
    fetches[0].wait()
    for half in range(halves):
        lanes = slice(half * LANES, (half + 1) * LANES)
        for i in range(3 * bins):
            columns[i : i + 1, :] = places[i, :, lanes]
        turned = jnp.transpose(columns[...])
        for i in range(3 * bins):
            spread[i, lanes, :] = jnp.broadcast_to(turned[:, i : i + 1], (LANES, LANES))
    for fetch in fetches[1:]:
        fetch.wait()

    sources[0] = jnp.zeros((8, LANES), jnp.float32)
    filled = jnp.int32(0)
    for dx in (-1, 0, 1):
        for dz in (-1, 0, 1):
            column_z = lax.rem(z + (dz + helpers), helpers)
            if (dx, dz) == (0, 0):
                column, weights = places, masses
            else:
                column, weights = (ref.at[SIDES.index((dx, dz))] for ref in (halo, mass_halo))
            for s in range(bins):
                live = all_counts[1 + dx, s, 0, column_z]
                shift = jnp.where(row == 0, float(dx), jnp.where(row == bins + 1, float(dz), 0.0))
                for t in range(bins):
                    below = links[0, t, z, (dx + 1) * 9 + (dz + 1) * 3] == s
                    above = links[0, t, z, (dx + 1) * 9 + (dz + 1) * 3 + 2] == s
                    along = jnp.where(below, -1.0, jnp.where(above, 1.0, 0.0)).astype(jnp.float32)
                    shift = jnp.where(row == 1 + t, along, shift)
                tile = filled // LANES
                turn = lax.rem(filled, LANES)
                kept = lane >= turn
                carried = sources[tile]
                for half in range(halves):
                    lanes = slice(half * LANES, (half + 1) * LANES)
                    line = [
                        jnp.broadcast_to(part, (8, LANES))
                        for part in [column[c * bins + s, :, lanes] for c in range(3)]
                        + [weights[s, :, lanes]]
                    ]
                    block = jnp.where(row == bins + 1, line[2], line[3])
                    block = jnp.where(row <= bins, line[1], block)
                    block = jnp.where(row == 0, line[0], block)
                    block = jnp.where(lane + half * LANES < live, block + shift, 0.0)
                    turned = pltpu.roll(block, turn, 1)
                    sources[tile + half] = carried + jnp.where(kept, turned, 0.0)
                    carried = jnp.where(kept, 0.0, turned)
                sources[tile + halves] = carried
                filled = filled + live
    used = (filled + LANES - 1) // LANES

    for t in range(bins):
        live = all_counts[1, t, 0, z]

        def work(group, carry):
            rows = pl.ds(pl.multiple_of(group * GROUP, GROUP), GROUP)
            targets = [spread[c * bins + t, rows, :] for c in range(3)]

            def add(first, size, sums):
                sums = list(sums)
                for k in range(size):
                    tile = first + k
                    sx = sources[tile, 0:1, :]
                    sy = sources[tile, 1 + t : 2 + t, :]
                    sz = sources[tile, bins + 1 : bins + 2, :]
                    mass = sources[tile, bins + 2 : bins + 3, :]
                    ex = sx - targets[0]
                    ey = sy - targets[1]
                    ez = sz - targets[2]
                    inverse = lax.rsqrt(ex * ex + ey * ey + (ez * ez + softening))
                    weight = (mass * inverse) * (inverse * inverse)
                    sums[0] = sums[0] + weight * ex
                    sums[1] = sums[1] + weight * ey
                    sums[2] = sums[2] + weight * ez
                return tuple(sums)

            sums = (jnp.zeros((GROUP, LANES), jnp.float32),) * 3
            done = jnp.int32(0)
            for size in TILES:
                rounds = (used - done) // size
                sums = lax.fori_loop(
                    0, rounds, lambda i, sums, d=done, n=size: add(d + i * n, n, sums), sums
                )
                done = done + rounds * size
            for c in range(3):
                totals[c * bins + t, rows, :] = sums[c]
            return carry

        lax.fori_loop(0, (live + GROUP - 1) // GROUP, work, 0)

    for half in range(halves):
        lanes = slice(half * LANES, (half + 1) * LANES)
        columns[...] = jnp.zeros_like(columns)
        for t in range(bins):

            @pl.when(all_counts[1, t, 0, z] > half * LANES)
            def _():
                found = columns[...]
                for c in range(3):
                    at = c * bins + t
                    found = jnp.where(
                        wide_lane == at, jnp.sum(totals[at, lanes, :], axis=1, keepdims=True), found
                    )
                columns[...] = found

        summed = jnp.transpose(columns[...])
        for t in range(bins):
            alive = lane[0:1] + half * LANES < all_counts[1, t, 0, z]
            for c in range(3):
                at = c * bins + t
                accel = jnp.where(alive, summed[at : at + 1] * (strength / slots), 0.0)
                speed = speeds[at, :, lanes] + time_step * accel
                speeds[at, :, lanes] = speed
                places[at, :, lanes] = places[at, :, lanes] + time_step * speed
    stores = [
        pltpu.make_async_copy(places, places_out, sems.at[0]),
        pltpu.make_async_copy(speeds, speeds_out, sems.at[1]),
    ]
    for store in stores:
        store.start()
    for store in stores:
        store.wait()


def on_device(positions, velocities, masses, counts, neighbours):
    bins, slots = positions.shape[3:]
    helpers = counts.shape[1]
    sides = len(SIDES)
    hbm = pl.BlockSpec(memory_space=pltpu.HBM)
    dma = pltpu.SemaphoreType.DMA

    def floats(*shape):
        return jax.ShapeDtypeStruct(shape, jnp.float32)

    places = positions.reshape(3 * bins, 1, slots)
    speeds = velocities.reshape(3 * bins, 1, slots)
    masses = masses.reshape(bins, 1, slots)
    counts = counts.transpose(2, 0, 1)
    links = neighbours.transpose(0, 2, 1, 3)

    halo, mass_halo, all_counts = pl.pallas_call(
        first_exchange,
        out_shape=(
            floats(sides, 3 * bins, 1, slots),
            floats(sides, bins, 1, slots),
            jax.ShapeDtypeStruct((3, bins, 1, helpers), jnp.int32),
        ),
        in_specs=[hbm] * 3,
        out_specs=(hbm,) * 3,
        scratch_shapes=[dma((sides,))] * 4 + [dma((3,))] * 2,
        compiler_params=pltpu.CompilerParams(collective_id=0, has_side_effects=True),
        name="first_exchange",
    )(places, masses, counts)

    exchange = pl.pallas_call(
        later_exchange,
        out_shape=floats(sides, 3 * bins, 1, slots),
        in_specs=[hbm],
        out_specs=hbm,
        scratch_shapes=[dma((sides,))] * 2,
        compiler_params=pltpu.CompilerParams(collective_id=1, has_side_effects=True),
        name="later_exchange",
    )

    tiles = (sides + 1) * bins * slots // LANES + slots // LANES + 1
    state = floats(3 * bins, 1, slots)

    step = pl.pallas_call(
        step_kernel,
        out_shape=(state, state),
        in_specs=[hbm] * 7,
        out_specs=(hbm, hbm),
        scratch_shapes=[
            pltpu.SMEM((3, bins, 1, helpers), jnp.int32),
            pltpu.SMEM(links.shape, jnp.int32),
            pltpu.VMEM(halo.shape, jnp.float32),
            pltpu.VMEM(mass_halo.shape, jnp.float32),
            pltpu.VMEM(state.shape, jnp.float32),
            pltpu.VMEM(masses.shape, jnp.float32),
            pltpu.VMEM(state.shape, jnp.float32),
            pltpu.VMEM((tiles, 8, LANES), jnp.float32),
            pltpu.VMEM((3 * bins, slots, LANES), jnp.float32),
            pltpu.VMEM((3 * bins, slots, LANES), jnp.float32),
            pltpu.VMEM((LANES, LANES), jnp.float32),
            dma((7,)),
        ],
        name="step",
    )
    for substep in range(SUBSTEPS):
        if substep > 0:
            halo = exchange(places)
        places, speeds = step(all_counts, links, halo, mass_halo, places, masses, speeds)
    return places.reshape(positions.shape), speeds.reshape(velocities.shape)


def solution(mesh):
    return jax.shard_map(
        on_device,
        mesh=mesh,
        in_specs=(
            P(None, "dom", "help", None, None),
            P(None, "dom", "help", None, None),
            P("dom", "help", None, None),
            P("dom", None, None),
            P("dom", None, None, None),
        ),
        out_specs=(P(None, "dom", "help", None, None), P(None, "dom", "help", None, None)),
        check_vma=False,
    )
```

```python
import jax
import jax.numpy as jnp
from jax import lax
from jax.experimental import pallas as pl
from jax.experimental.pallas import tpu as pltpu
from jax.sharding import PartitionSpec as P

SUBSTEPS = 3
LANES = 128
GROUPS = (32, 16, 8)
TILES = (16, 8, 4, 2, 1)

softening = 0.25
strength = 4.0
time_step = 0.2

SIDES = [(dx, dz) for dx in (-1, 0, 1) for dz in (-1, 0, 1) if (dx, dz) != (0, 0)]


def partner(dx, dz):
    def at(axis, step):
        count = lax.axis_size(axis)
        return lax.rem(lax.axis_index(axis) + (step + count), count)

    return {"dom": at("dom", dx), "help": at("help", dz)}


def greet():
    barrier = pltpu.get_barrier_semaphore()
    for dx, dz in SIDES:
        pl.semaphore_signal(
            barrier, inc=1, device_id=partner(dx, dz), device_id_type=pl.DeviceIdType.MESH
        )
    pl.semaphore_wait(barrier, len(SIDES))


def column_copies(column, halo, send_sem, recv_sem):
    last = len(SIDES) - 1
    return [
        pltpu.make_async_remote_copy(
            src_ref=column,
            dst_ref=halo.at[last - index],
            send_sem=send_sem.at[index],
            recv_sem=recv_sem.at[last - index],
            device_id=partner(dx, dz),
            device_id_type=pl.DeviceIdType.MESH,
        )
        for index, (dx, dz) in enumerate(SIDES)
    ]


def first_exchange(places, masses, counts, halo, mass_halo, all_counts, *sems):
    greet()
    copies = column_copies(places, halo, sems[0], sems[1])
    copies += column_copies(masses, mass_halo, sems[2], sems[3])
    for dx in (-1, 1):
        copies.append(
            pltpu.make_async_remote_copy(
                src_ref=counts,
                dst_ref=all_counts.at[1 - dx],
                send_sem=sems[4].at[1 + dx],
                recv_sem=sems[5].at[1 - dx],
                device_id=partner(dx, 0),
                device_id_type=pl.DeviceIdType.MESH,
            )
        )
    copies.append(pltpu.make_async_copy(counts, all_counts.at[1], sems[4].at[1]))
    for copy in copies:
        copy.start()
    for copy in copies:
        copy.wait()


def later_exchange(places, halo, send_sem, recv_sem):
    greet()
    copies = column_copies(places, halo, send_sem, recv_sem)
    for copy in copies:
        copy.start()
    for copy in copies:
        copy.wait()


def step_kernel(
    counts_in, links_in, halo_in, mass_halo_in, places_in, masses_in, speeds_in,
    places_out, speeds_out, all_counts, links, halo, mass_halo, places, masses, speeds,
    sources, spread, totals, columns, sems,
):
    pairs = [
        (places_in, places),
        (counts_in, all_counts),
        (links_in, links),
        (halo_in, halo),
        (mass_halo_in, mass_halo),
        (masses_in, masses),
        (speeds_in, speeds),
    ]
    fetches = [
        pltpu.make_async_copy(there, here, sems.at[i]) for i, (there, here) in enumerate(pairs)
    ]
    for fetch in fetches:
        fetch.start()
    bins = masses.shape[0]
    helpers = all_counts.shape[3]
    slots = masses.shape[2]
    halves = slots // LANES
    z = lax.axis_index("help")
    lane = lax.broadcasted_iota(jnp.int32, (8, LANES), 1)
    row = lax.broadcasted_iota(jnp.int32, (8, LANES), 0)
    wide_lane = lax.broadcasted_iota(jnp.int32, (LANES, LANES), 1)

    columns[...] = jnp.zeros_like(columns)
    fetches[0].wait()
    for half in range(halves):
        lanes = slice(half * LANES, (half + 1) * LANES)
        for i in range(3 * bins):
            columns[i : i + 1, :] = places[i, :, lanes]
        turned = jnp.transpose(columns[...])
        for i in range(3 * bins):
            spread[i, lanes, :] = jnp.broadcast_to(turned[:, i : i + 1], (LANES, LANES))
    for fetch in fetches[1:]:
        fetch.wait()

    sources[0] = jnp.zeros((8, LANES), jnp.float32)
    filled = jnp.int32(0)
    for dx in (-1, 0, 1):
        for dz in (-1, 0, 1):
            column_z = lax.rem(z + (dz + helpers), helpers)
            if (dx, dz) == (0, 0):
                column, weights = places, masses
            else:
                column, weights = (ref.at[SIDES.index((dx, dz))] for ref in (halo, mass_halo))
            for s in range(bins):
                live = all_counts[1 + dx, s, 0, column_z]
                shift = jnp.where(row == 0, float(dx), jnp.where(row == bins + 1, float(dz), 0.0))
                for t in range(bins):
                    below = links[0, t, z, (dx + 1) * 9 + (dz + 1) * 3] == s
                    above = links[0, t, z, (dx + 1) * 9 + (dz + 1) * 3 + 2] == s
                    along = jnp.where(below, -1.0, jnp.where(above, 1.0, 0.0)).astype(jnp.float32)
                    shift = jnp.where(row == 1 + t, along, shift)
                tile = filled // LANES
                turn = lax.rem(filled, LANES)
                kept = lane >= turn
                carried = sources[tile]
                for half in range(halves):
                    lanes = slice(half * LANES, (half + 1) * LANES)
                    line = [
                        jnp.broadcast_to(part, (8, LANES))
                        for part in [column[c * bins + s, :, lanes] for c in range(3)]
                        + [weights[s, :, lanes]]
                    ]
                    block = jnp.where(row == bins + 1, line[2], line[3])
                    block = jnp.where(row <= bins, line[1], block)
                    block = jnp.where(row == 0, line[0], block)
                    block = jnp.where(lane + half * LANES < live, block + shift, 0.0)
                    turned = pltpu.roll(block, turn, 1)
                    sources[tile + half] = carried + jnp.where(kept, turned, 0.0)
                    carried = jnp.where(kept, 0.0, turned)
                sources[tile + halves] = carried
                filled = filled + live
    used = (filled + LANES - 1) // LANES

    def one_bin(t, carry):
        def work(start, size):
            rows = pl.ds(pl.multiple_of(start, 8), size)
            targets = [spread[c * bins + t, rows, :] for c in range(3)]

            def add(first, count, sums):
                sums = list(sums)
                for k in range(count):
                    tile = first + k
                    sx = sources[tile, 0:1, :]
                    sy = sources[tile, pl.ds(1 + t, 1), :]
                    sz = sources[tile, bins + 1 : bins + 2, :]
                    mass = sources[tile, bins + 2 : bins + 3, :]
                    ex = sx - targets[0]
                    ey = sy - targets[1]
                    ez = sz - targets[2]
                    inverse = lax.rsqrt(ex * ex + ey * ey + (ez * ez + softening))
                    weight = (mass * inverse) * (inverse * inverse)
                    sums[0] = sums[0] + weight * ex
                    sums[1] = sums[1] + weight * ey
                    sums[2] = sums[2] + weight * ez
                return tuple(sums)

            sums = (jnp.zeros((size, LANES), jnp.float32),) * 3
            done = jnp.int32(0)
            for count in TILES:
                rounds = (used - done) // count
                sums = lax.fori_loop(
                    0, rounds, lambda i, sums, d=done, n=count: add(d + i * n, n, sums), sums
                )
                done = done + rounds * count
            for c in range(3):
                totals[c * bins + t, rows, :] = sums[c]

        live = (all_counts[1, t, 0, z] + 7) // 8 * 8
        first = jnp.int32(0)
        for size in GROUPS:
            groups = (live - first) // size

            def one_group(group, carry, first=first, size=size):
                work(first + group * size, size)
                return carry

            lax.fori_loop(0, groups, one_group, 0)
            first = first + groups * size
        return carry

    lax.fori_loop(0, bins, one_bin, 0)

    for half in range(halves):
        lanes = slice(half * LANES, (half + 1) * LANES)
        columns[...] = jnp.zeros_like(columns)
        for t in range(bins):

            @pl.when(all_counts[1, t, 0, z] > half * LANES)
            def _():
                found = columns[...]
                for c in range(3):
                    at = c * bins + t
                    found = jnp.where(
                        wide_lane == at, jnp.sum(totals[at, lanes, :], axis=1, keepdims=True), found
                    )
                columns[...] = found

        summed = jnp.transpose(columns[...])
        for t in range(bins):
            alive = lane[0:1] + half * LANES < all_counts[1, t, 0, z]
            for c in range(3):
                at = c * bins + t
                accel = jnp.where(alive, summed[at : at + 1] * (strength / slots), 0.0)
                speed = speeds[at, :, lanes] + time_step * accel
                speeds[at, :, lanes] = speed
                places[at, :, lanes] = places[at, :, lanes] + time_step * speed
    stores = [
        pltpu.make_async_copy(places, places_out, sems.at[0]),
        pltpu.make_async_copy(speeds, speeds_out, sems.at[1]),
    ]
    for store in stores:
        store.start()
    for store in stores:
        store.wait()


def on_device(positions, velocities, masses, counts, neighbours):
    bins, slots = positions.shape[3:]
    helpers = counts.shape[1]
    sides = len(SIDES)
    hbm = pl.BlockSpec(memory_space=pltpu.HBM)
    dma = pltpu.SemaphoreType.DMA

    def floats(*shape):
        return jax.ShapeDtypeStruct(shape, jnp.float32)

    places = positions.reshape(3 * bins, 1, slots)
    speeds = velocities.reshape(3 * bins, 1, slots)
    masses = masses.reshape(bins, 1, slots)
    counts = counts.transpose(2, 0, 1)
    links = neighbours.transpose(0, 2, 1, 3)

    halo, mass_halo, all_counts = pl.pallas_call(
        first_exchange,
        out_shape=(
            floats(sides, 3 * bins, 1, slots),
            floats(sides, bins, 1, slots),
            jax.ShapeDtypeStruct((3, bins, 1, helpers), jnp.int32),
        ),
        in_specs=[hbm] * 3,
        out_specs=(hbm,) * 3,
        scratch_shapes=[dma((sides,))] * 4 + [dma((3,))] * 2,
        compiler_params=pltpu.CompilerParams(collective_id=0, has_side_effects=True),
        name="first_exchange",
    )(places, masses, counts)

    exchange = pl.pallas_call(
        later_exchange,
        out_shape=floats(sides, 3 * bins, 1, slots),
        in_specs=[hbm],
        out_specs=hbm,
        scratch_shapes=[dma((sides,))] * 2,
        compiler_params=pltpu.CompilerParams(collective_id=1, has_side_effects=True),
        name="later_exchange",
    )

    tiles = (sides + 1) * bins * slots // LANES + slots // LANES + 1
    state = floats(3 * bins, 1, slots)

    step = pl.pallas_call(
        step_kernel,
        out_shape=(state, state),
        in_specs=[hbm] * 7,
        out_specs=(hbm, hbm),
        scratch_shapes=[
            pltpu.SMEM((3, bins, 1, helpers), jnp.int32),
            pltpu.SMEM(links.shape, jnp.int32),
            pltpu.VMEM(halo.shape, jnp.float32),
            pltpu.VMEM(mass_halo.shape, jnp.float32),
            pltpu.VMEM(state.shape, jnp.float32),
            pltpu.VMEM(masses.shape, jnp.float32),
            pltpu.VMEM(state.shape, jnp.float32),
            pltpu.VMEM((tiles, 8, LANES), jnp.float32),
            pltpu.VMEM((3 * bins, slots, LANES), jnp.float32),
            pltpu.VMEM((3 * bins, slots, LANES), jnp.float32),
            pltpu.VMEM((LANES, LANES), jnp.float32),
            dma((7,)),
        ],
        name="step",
    )
    for substep in range(SUBSTEPS):
        if substep > 0:
            halo = exchange(places)
        places, speeds = step(all_counts, links, halo, mass_halo, places, masses, speeds)
    return places.reshape(positions.shape), speeds.reshape(velocities.shape)


def solution(mesh):
    return jax.shard_map(
        on_device,
        mesh=mesh,
        in_specs=(
            P(None, "dom", "help", None, None),
            P(None, "dom", "help", None, None),
            P("dom", "help", None, None),
            P("dom", None, None),
            P("dom", None, None, None),
        ),
        out_specs=(P(None, "dom", "help", None, None), P(None, "dom", "help", None, None)),
        check_vma=False,
    )
```

```python
import jax
import jax.numpy as jnp
from jax import lax
from jax.experimental import pallas as pl
from jax.experimental.pallas import tpu as pltpu
from jax.sharding import PartitionSpec as P

SUBSTEPS = 3
LANES = 128
GROUPS = (32, 16, 8)
TILES = (16, 8, 4, 2, 1)

softening = 0.25
strength = 4.0
time_step = 0.2

SIDES = [(dx, dz) for dx in (-1, 0, 1) for dz in (-1, 0, 1) if (dx, dz) != (0, 0)]


def partner(dx, dz):
    def at(axis, step):
        count = lax.axis_size(axis)
        return lax.rem(lax.axis_index(axis) + (step + count), count)

    return {"dom": at("dom", dx), "help": at("help", dz)}


def greet():
    barrier = pltpu.get_barrier_semaphore()
    for dx, dz in SIDES:
        pl.semaphore_signal(
            barrier, inc=1, device_id=partner(dx, dz), device_id_type=pl.DeviceIdType.MESH
        )
    pl.semaphore_wait(barrier, len(SIDES))


def column_copies(column, halo, send_sem, recv_sem):
    last = len(SIDES) - 1
    return [
        pltpu.make_async_remote_copy(
            src_ref=column,
            dst_ref=halo.at[last - index],
            send_sem=send_sem.at[index],
            recv_sem=recv_sem.at[last - index],
            device_id=partner(dx, dz),
            device_id_type=pl.DeviceIdType.MESH,
        )
        for index, (dx, dz) in enumerate(SIDES)
    ]


def lane_and_row():
    shape = (8, LANES)
    return lax.broadcasted_iota(jnp.int32, shape, 1), lax.broadcasted_iota(jnp.int32, shape, 0)


def bin_shift(links, z, dx, dz, s, bins):
    _, row = lane_and_row()
    shift = jnp.where(row == 0, float(dx), jnp.where(row == bins + 1, float(dz), 0.0))
    for t in range(bins):
        below = links[0, t, z, (dx + 1) * 9 + (dz + 1) * 3] == s
        above = links[0, t, z, (dx + 1) * 9 + (dz + 1) * 3 + 2] == s
        along = jnp.where(below, -1.0, jnp.where(above, 1.0, 0.0)).astype(jnp.float32)
        shift = jnp.where(row == 1 + t, along, shift)
    return shift


def source_block(column, weights, s, half, bins, shift, live):
    lane, row = lane_and_row()
    lanes = slice(half * LANES, (half + 1) * LANES)
    line = [
        jnp.broadcast_to(part, (8, LANES))
        for part in [column[c * bins + s, :, lanes] for c in range(3)] + [weights[s, :, lanes]]
    ]
    block = jnp.where(row == bins + 1, line[2], line[3])
    block = jnp.where(row <= bins, line[1], block)
    block = jnp.where(row == 0, line[0], block)
    return jnp.where(lane + half * LANES < live, block + shift, 0.0)


def spread_targets(places, columns, spread):
    columns[...] = jnp.zeros_like(columns)
    rows, slots = spread.shape[:2]
    for half in range(slots // LANES):
        lanes = slice(half * LANES, (half + 1) * LANES)
        for i in range(rows):
            columns[i : i + 1, :] = places[i, :, lanes]
        turned = jnp.transpose(columns[...])
        for i in range(rows):
            spread[i, lanes, :] = jnp.broadcast_to(turned[:, i : i + 1], (LANES, LANES))


def add_pairs(sources, first, count, t, bins, targets, sums):
    sums = list(sums)
    for k in range(count):
        tile = first + k
        sx = sources[tile, 0:1, :]
        sy = sources[tile, pl.ds(1 + t, 1), :]
        sz = sources[tile, bins + 1 : bins + 2, :]
        mass = sources[tile, bins + 2 : bins + 3, :]
        ex = sx - targets[0]
        ey = sy - targets[1]
        ez = sz - targets[2]
        inverse = lax.rsqrt(ex * ex + ey * ey + (ez * ez + softening))
        weight = (mass * inverse) * (inverse * inverse)
        sums[0] = sums[0] + weight * ex
        sums[1] = sums[1] + weight * ey
        sums[2] = sums[2] + weight * ez
    return tuple(sums)


def own_column(places, masses, counts, links, forces, sources, spread, totals, columns):
    bins, _, slots = masses.shape
    halves = slots // LANES
    z = lax.axis_index("help")
    for s in range(bins):
        shift = bin_shift(links, z, 0, 0, s, bins)
        for half in range(halves):
            sources[s * halves + half] = source_block(
                places, masses, s, half, bins, shift, counts[s, 0, z]
            )
    spread_targets(places, columns, spread)
    groups = slots // GROUPS[0]

    def work(group, carry):
        t = group // groups
        rows = pl.ds(pl.multiple_of(group % groups * GROUPS[0], GROUPS[0]), GROUPS[0])
        targets = [spread[c * bins + t, rows, :] for c in range(3)]
        zero = jnp.zeros((GROUPS[0], LANES), jnp.float32)
        sums = add_pairs(sources, 0, bins * halves, t, bins, targets, (zero, zero, zero))
        for c in range(3):
            totals[c * bins + t, rows, :] = sums[c]
        return carry

    lax.fori_loop(0, bins * groups, work, 0)
    wide_lane = lax.broadcasted_iota(jnp.int32, (LANES, LANES), 1)
    for half in range(halves):
        lanes = slice(half * LANES, (half + 1) * LANES)
        found = jnp.zeros((LANES, LANES), jnp.float32)
        for at in range(3 * bins):
            found = jnp.where(
                wide_lane == at, jnp.sum(totals[at, lanes, :], axis=1, keepdims=True), found
            )
        summed = jnp.transpose(found)
        for at in range(3 * bins):
            forces[at, :, lanes] = summed[at : at + 1]


def exchange_beside_work(copies, inputs, forces_out, local, work, sems):
    fetches = [
        pltpu.make_async_copy(there, here, sems.at[i])
        for i, (there, here) in enumerate(zip(inputs, local[:4]))
    ]
    for fetch in fetches:
        fetch.start()
    greet()
    for copy in copies:
        copy.start()
    for fetch in fetches:
        fetch.wait()
    own_column(*local, *work)
    store = pltpu.make_async_copy(local[4], forces_out, sems.at[4])
    store.start()
    for copy in copies:
        copy.wait()
    store.wait()


def first_exchange(places, masses, counts, links, halo, mass_halo, all_counts, forces, *rest):
    sems, local, work, fetch_sems = rest[:6], rest[6:11], rest[11:15], rest[15]
    copies = column_copies(places, halo, sems[0], sems[1])
    copies += column_copies(masses, mass_halo, sems[2], sems[3])
    for dx in (-1, 1):
        copies.append(
            pltpu.make_async_remote_copy(
                src_ref=counts,
                dst_ref=all_counts.at[1 - dx],
                send_sem=sems[4].at[1 + dx],
                recv_sem=sems[5].at[1 - dx],
                device_id=partner(dx, 0),
                device_id_type=pl.DeviceIdType.MESH,
            )
        )
    copies.append(pltpu.make_async_copy(counts, all_counts.at[1], sems[4].at[1]))
    exchange_beside_work(copies, (places, masses, counts, links), forces, local, work, fetch_sems)


def later_exchange(places, masses, counts, links, halo, forces, *rest):
    sems, local, work, fetch_sems = rest[:2], rest[2:7], rest[7:11], rest[11]
    copies = column_copies(places, halo, sems[0], sems[1])
    exchange_beside_work(copies, (places, masses, counts, links), forces, local, work, fetch_sems)


def step_kernel(
    counts_in, links_in, halo_in, mass_halo_in, places_in, forces_in, speeds_in,
    places_out, speeds_out, all_counts, links, halo, mass_halo, places, forces, speeds,
    sources, spread, totals, columns, sems,
):
    pairs = [
        (places_in, places),
        (counts_in, all_counts),
        (links_in, links),
        (halo_in, halo),
        (mass_halo_in, mass_halo),
        (forces_in, forces),
        (speeds_in, speeds),
    ]
    fetches = [
        pltpu.make_async_copy(there, here, sems.at[i]) for i, (there, here) in enumerate(pairs)
    ]
    for fetch in fetches:
        fetch.start()
    bins = mass_halo.shape[1]
    helpers = all_counts.shape[3]
    slots = mass_halo.shape[3]
    halves = slots // LANES
    z = lax.axis_index("help")
    lane, _ = lane_and_row()
    wide_lane = lax.broadcasted_iota(jnp.int32, (LANES, LANES), 1)

    fetches[0].wait()
    spread_targets(places, columns, spread)
    for fetch in fetches[1:]:
        fetch.wait()

    sources[0] = jnp.zeros((8, LANES), jnp.float32)
    filled = jnp.int32(0)
    for index, (dx, dz) in enumerate(SIDES):
        column_z = lax.rem(z + (dz + helpers), helpers)
        for s in range(bins):
            live = all_counts[1 + dx, s, 0, column_z]
            shift = bin_shift(links, z, dx, dz, s, bins)
            tile = filled // LANES
            turn = lax.rem(filled, LANES)
            kept = lane >= turn
            carried = sources[tile]
            for half in range(halves):
                block = source_block(
                    halo.at[index], mass_halo.at[index], s, half, bins, shift, live
                )
                turned = pltpu.roll(block, turn, 1)
                sources[tile + half] = carried + jnp.where(kept, turned, 0.0)
                carried = jnp.where(kept, 0.0, turned)
            sources[tile + halves] = carried
            filled = filled + live
    used = (filled + LANES - 1) // LANES

    def one_bin(t, carry):
        def work(start, size):
            rows = pl.ds(pl.multiple_of(start, 8), size)
            targets = [spread[c * bins + t, rows, :] for c in range(3)]

            sums = (jnp.zeros((size, LANES), jnp.float32),) * 3
            done = jnp.int32(0)
            for count in TILES:
                rounds = (used - done) // count
                sums = lax.fori_loop(
                    0, rounds, lambda i, sums, d=done, n=count: add_pairs(
                        sources, d + i * n, n, t, bins, targets, sums
                    ), sums
                )
                done = done + rounds * count
            for c in range(3):
                totals[c * bins + t, rows, :] = sums[c]

        live = (all_counts[1, t, 0, z] + 7) // 8 * 8
        first = jnp.int32(0)
        for size in GROUPS:
            groups = (live - first) // size

            def one_group(group, carry, first=first, size=size):
                work(first + group * size, size)
                return carry

            lax.fori_loop(0, groups, one_group, 0)
            first = first + groups * size
        return carry

    lax.fori_loop(0, bins, one_bin, 0)

    for half in range(halves):
        lanes = slice(half * LANES, (half + 1) * LANES)
        columns[...] = jnp.zeros_like(columns)
        for t in range(bins):

            @pl.when(all_counts[1, t, 0, z] > half * LANES)
            def _():
                found = columns[...]
                for c in range(3):
                    at = c * bins + t
                    found = jnp.where(
                        wide_lane == at, jnp.sum(totals[at, lanes, :], axis=1, keepdims=True), found
                    )
                columns[...] = found

        summed = jnp.transpose(columns[...])
        for t in range(bins):
            alive = lane[0:1] + half * LANES < all_counts[1, t, 0, z]
            for c in range(3):
                at = c * bins + t
                force = summed[at : at + 1] + forces[at, :, lanes]
                accel = jnp.where(alive, force * (strength / slots), 0.0)
                speed = speeds[at, :, lanes] + time_step * accel
                speeds[at, :, lanes] = speed
                places[at, :, lanes] = places[at, :, lanes] + time_step * speed
    stores = [
        pltpu.make_async_copy(places, places_out, sems.at[0]),
        pltpu.make_async_copy(speeds, speeds_out, sems.at[1]),
    ]
    for store in stores:
        store.start()
    for store in stores:
        store.wait()


def on_device(positions, velocities, masses, counts, neighbours):
    bins, slots = positions.shape[3:]
    helpers = counts.shape[1]
    sides = len(SIDES)
    hbm = pl.BlockSpec(memory_space=pltpu.HBM)
    dma = pltpu.SemaphoreType.DMA

    def floats(*shape):
        return jax.ShapeDtypeStruct(shape, jnp.float32)

    places = positions.reshape(3 * bins, 1, slots)
    speeds = velocities.reshape(3 * bins, 1, slots)
    masses = masses.reshape(bins, 1, slots)
    counts = counts.transpose(2, 0, 1)
    links = neighbours.transpose(0, 2, 1, 3)

    state = floats(3 * bins, 1, slots)
    work = [
        pltpu.VMEM(state.shape, jnp.float32),
        pltpu.VMEM(masses.shape, jnp.float32),
        pltpu.SMEM(counts.shape, jnp.int32),
        pltpu.SMEM(links.shape, jnp.int32),
        pltpu.VMEM(state.shape, jnp.float32),
        pltpu.VMEM((bins * slots // LANES, 8, LANES), jnp.float32),
        pltpu.VMEM((3 * bins, slots, LANES), jnp.float32),
        pltpu.VMEM((3 * bins, slots, LANES), jnp.float32),
        pltpu.VMEM((LANES, LANES), jnp.float32),
        dma((5,)),
    ]
    halo, mass_halo, all_counts, forces = pl.pallas_call(
        first_exchange,
        out_shape=(
            floats(sides, 3 * bins, 1, slots),
            floats(sides, bins, 1, slots),
            jax.ShapeDtypeStruct((3, bins, 1, helpers), jnp.int32),
            state,
        ),
        in_specs=[hbm] * 4,
        out_specs=(hbm,) * 4,
        scratch_shapes=[dma((sides,))] * 4 + [dma((3,))] * 2 + work,
        compiler_params=pltpu.CompilerParams(collective_id=0, has_side_effects=True),
        name="first_exchange",
    )(places, masses, counts, links)

    exchange = pl.pallas_call(
        later_exchange,
        out_shape=(floats(sides, 3 * bins, 1, slots), state),
        in_specs=[hbm] * 4,
        out_specs=(hbm, hbm),
        scratch_shapes=[dma((sides,))] * 2 + work,
        compiler_params=pltpu.CompilerParams(collective_id=1, has_side_effects=True),
        name="later_exchange",
    )

    tiles = sides * bins * slots // LANES + slots // LANES + 1
    step = pl.pallas_call(
        step_kernel,
        out_shape=(state, state),
        in_specs=[hbm] * 7,
        out_specs=(hbm, hbm),
        scratch_shapes=[
            pltpu.SMEM((3, bins, 1, helpers), jnp.int32),
            pltpu.SMEM(links.shape, jnp.int32),
            pltpu.VMEM(halo.shape, jnp.float32),
            pltpu.VMEM(mass_halo.shape, jnp.float32),
            pltpu.VMEM(state.shape, jnp.float32),
            pltpu.VMEM(state.shape, jnp.float32),
            pltpu.VMEM(state.shape, jnp.float32),
            pltpu.VMEM((tiles, 8, LANES), jnp.float32),
            pltpu.VMEM((3 * bins, slots, LANES), jnp.float32),
            pltpu.VMEM((3 * bins, slots, LANES), jnp.float32),
            pltpu.VMEM((LANES, LANES), jnp.float32),
            dma((7,)),
        ],
        name="step",
    )
    for substep in range(SUBSTEPS):
        if substep > 0:
            halo, forces = exchange(places, masses, counts, links)
        places, speeds = step(all_counts, links, halo, mass_halo, places, forces, speeds)
    return places.reshape(positions.shape), speeds.reshape(velocities.shape)


def solution(mesh):
    return jax.shard_map(
        on_device,
        mesh=mesh,
        in_specs=(
            P(None, "dom", "help", None, None),
            P(None, "dom", "help", None, None),
            P("dom", "help", None, None),
            P("dom", None, None),
            P("dom", None, None, None),
        ),
        out_specs=(P(None, "dom", "help", None, None), P(None, "dom", "help", None, None)),
        check_vma=False,
    )
```

```python
import jax
import jax.numpy as jnp
from jax import lax
from jax.experimental import pallas as pl
from jax.experimental.pallas import tpu as pltpu
from jax.sharding import PartitionSpec as P

SUBSTEPS = 3
LANES = 128
GROUPS = (32, 16, 8)
TILES = (16, 8, 4, 2, 1)

softening = 0.25
strength = 4.0
time_step = 0.2

SIDES = [(dx, dz) for dx in (-1, 0, 1) for dz in (-1, 0, 1) if (dx, dz) != (0, 0)]


def partner(dx, dz):
    def at(axis, step):
        count = lax.axis_size(axis)
        return lax.rem(lax.axis_index(axis) + (step + count), count)

    return {"dom": at("dom", dx), "help": at("help", dz)}


def greet():
    barrier = pltpu.get_barrier_semaphore()
    for dx, dz in SIDES:
        pl.semaphore_signal(
            barrier, inc=1, device_id=partner(dx, dz), device_id_type=pl.DeviceIdType.MESH
        )
    pl.semaphore_wait(barrier, len(SIDES))


def column_copies(column, halo, send_sem, recv_sem):
    last = len(SIDES) - 1
    return [
        pltpu.make_async_remote_copy(
            src_ref=column,
            dst_ref=halo.at[last - index],
            send_sem=send_sem.at[index],
            recv_sem=recv_sem.at[last - index],
            device_id=partner(dx, dz),
            device_id_type=pl.DeviceIdType.MESH,
        )
        for index, (dx, dz) in enumerate(SIDES)
    ]


def lane_and_row():
    shape = (8, LANES)
    return lax.broadcasted_iota(jnp.int32, shape, 1), lax.broadcasted_iota(jnp.int32, shape, 0)


def bin_shift(links, z, dx, dz, s, bins):
    _, row = lane_and_row()
    shift = jnp.where(row == 0, float(dx), jnp.where(row == bins + 1, float(dz), 0.0))
    for t in range(bins):
        below = links[0, t, z, (dx + 1) * 9 + (dz + 1) * 3] == s
        above = links[0, t, z, (dx + 1) * 9 + (dz + 1) * 3 + 2] == s
        along = jnp.where(below, -1.0, jnp.where(above, 1.0, 0.0)).astype(jnp.float32)
        shift = jnp.where(row == 1 + t, along, shift)
    return shift


def source_block(column, weights, s, half, bins, shift, live):
    lane, row = lane_and_row()
    lanes = slice(half * LANES, (half + 1) * LANES)
    line = [
        jnp.broadcast_to(part, (8, LANES))
        for part in [column[c * bins + s, :, lanes] for c in range(3)] + [weights[s, :, lanes]]
    ]
    block = jnp.where(row == bins + 1, line[2], line[3])
    block = jnp.where(row <= bins, line[1], block)
    block = jnp.where(row == 0, line[0], block)
    return jnp.where(lane + half * LANES < live, block + shift, 0.0)


def spread_targets(places, columns, spread):
    columns[...] = jnp.zeros_like(columns)
    rows, slots = spread.shape[:2]
    for half in range(slots // LANES):
        lanes = slice(half * LANES, (half + 1) * LANES)
        for i in range(rows):
            columns[i : i + 1, :] = places[i, :, lanes]
        turned = jnp.transpose(columns[...])
        for i in range(rows):
            spread[i, lanes, :] = jnp.broadcast_to(turned[:, i : i + 1], (LANES, LANES))


def add_pairs(sources, first, count, t, bins, targets, sums):
    sums = list(sums)
    for k in range(count):
        tile = first + k
        sx = sources[tile, 0:1, :]
        sy = sources[tile, pl.ds(1 + t, 1), :]
        sz = sources[tile, bins + 1 : bins + 2, :]
        mass = sources[tile, bins + 2 : bins + 3, :]
        ex = sx - targets[0]
        ey = sy - targets[1]
        ez = sz - targets[2]
        inverse = lax.rsqrt(ex * ex + ey * ey + (ez * ez + softening))
        weight = (mass * inverse) * (inverse * inverse)
        sums[0] = sums[0] + weight * ex
        sums[1] = sums[1] + weight * ey
        sums[2] = sums[2] + weight * ez
    return tuple(sums)


def own_column(places, masses, counts, links, forces, sources, spread, totals, columns):
    bins, _, slots = masses.shape
    halves = slots // LANES
    z = lax.axis_index("help")
    for s in range(bins):
        shift = bin_shift(links, z, 0, 0, s, bins)
        for half in range(halves):
            sources[s * halves + half] = source_block(
                places, masses, s, half, bins, shift, counts[s, 0, z]
            )
    spread_targets(places, columns, spread)
    groups = slots // GROUPS[0]

    def work(group, carry):
        t = group // groups
        rows = pl.ds(pl.multiple_of(group % groups * GROUPS[0], GROUPS[0]), GROUPS[0])
        targets = [spread[c * bins + t, rows, :] for c in range(3)]
        zero = jnp.zeros((GROUPS[0], LANES), jnp.float32)
        sums = add_pairs(sources, 0, bins * halves, t, bins, targets, (zero, zero, zero))
        for c in range(3):
            totals[c * bins + t, rows, :] = sums[c]
        return carry

    lax.fori_loop(0, bins * groups, work, 0)
    wide_lane = lax.broadcasted_iota(jnp.int32, (LANES, LANES), 1)
    for half in range(halves):
        lanes = slice(half * LANES, (half + 1) * LANES)
        found = jnp.zeros((LANES, LANES), jnp.float32)
        for at in range(3 * bins):
            found = jnp.where(
                wide_lane == at, jnp.sum(totals[at, lanes, :], axis=1, keepdims=True), found
            )
        summed = jnp.transpose(found)
        for at in range(3 * bins):
            forces[at, :, lanes] = summed[at : at + 1]


def exchange_beside_work(copies, inputs, forces_out, local, work, sems):
    fetches = [
        pltpu.make_async_copy(there, here, sems.at[i])
        for i, (there, here) in enumerate(zip(inputs, local[:4]))
    ]
    for fetch in fetches:
        fetch.start()
    greet()
    for copy in copies:
        copy.start()
    for fetch in fetches:
        fetch.wait()
    own_column(*local, *work)
    store = pltpu.make_async_copy(local[4], forces_out, sems.at[4])
    store.start()
    for copy in copies:
        copy.wait()
    store.wait()


def first_exchange(places, masses, counts, links, halo, mass_halo, all_counts, forces, *rest):
    sems, local, work, fetch_sems = rest[:6], rest[6:11], rest[11:15], rest[15]
    copies = column_copies(places, halo, sems[0], sems[1])
    copies += column_copies(masses, mass_halo, sems[2], sems[3])
    for dx in (-1, 1):
        copies.append(
            pltpu.make_async_remote_copy(
                src_ref=counts,
                dst_ref=all_counts.at[1 - dx],
                send_sem=sems[4].at[1 + dx],
                recv_sem=sems[5].at[1 - dx],
                device_id=partner(dx, 0),
                device_id_type=pl.DeviceIdType.MESH,
            )
        )
    copies.append(pltpu.make_async_copy(counts, all_counts.at[1], sems[4].at[1]))
    exchange_beside_work(copies, (places, masses, counts, links), forces, local, work, fetch_sems)


def later_exchange(places, masses, counts, links, halo, forces, *rest):
    sems, local, work, fetch_sems = rest[:2], rest[2:7], rest[7:11], rest[11]
    copies = column_copies(places, halo, sems[0], sems[1])
    exchange_beside_work(copies, (places, masses, counts, links), forces, local, work, fetch_sems)


def step_kernel(
    counts_in, links_in, halo_in, mass_halo_in, places_in, forces_in, speeds_in,
    places_out, speeds_out, all_counts, links, halo, mass_halo, places, forces, speeds,
    sources, spread, totals, columns, sems,
):
    pairs = [
        (places_in, places),
        (counts_in, all_counts),
        (links_in, links),
        (halo_in, halo),
        (mass_halo_in, mass_halo),
        (forces_in, forces),
        (speeds_in, speeds),
    ]
    fetches = [
        pltpu.make_async_copy(there, here, sems.at[i]) for i, (there, here) in enumerate(pairs)
    ]
    for fetch in fetches:
        fetch.start()
    bins = mass_halo.shape[1]
    helpers = all_counts.shape[3]
    slots = mass_halo.shape[3]
    halves = slots // LANES
    z = lax.axis_index("help")
    lane, _ = lane_and_row()
    wide_lane = lax.broadcasted_iota(jnp.int32, (LANES, LANES), 1)

    for fetch in fetches:
        fetch.wait()
    spread_targets(places, columns, spread)

    sources[0] = jnp.zeros((8, LANES), jnp.float32)
    filled = jnp.int32(0)
    for index, (dx, dz) in enumerate(SIDES):
        column_z = lax.rem(z + (dz + helpers), helpers)
        for s in range(bins):
            live = all_counts[1 + dx, s, 0, column_z]
            shift = bin_shift(links, z, dx, dz, s, bins)
            tile = filled // LANES
            turn = lax.rem(filled, LANES)
            kept = lane >= turn
            carried = sources[tile]
            for half in range(halves):
                block = source_block(
                    halo.at[index], mass_halo.at[index], s, half, bins, shift, live
                )
                turned = pltpu.roll(block, turn, 1)
                sources[tile + half] = carried + jnp.where(kept, turned, 0.0)
                carried = jnp.where(kept, 0.0, turned)
            sources[tile + halves] = carried
            filled = filled + live
    used = (filled + LANES - 1) // LANES
    runs = []
    done = jnp.int32(0)
    for count in TILES:
        rounds = (used - done) // count
        runs.append((done, count, rounds))
        done = done + rounds * count

    def one_bin(t, carry):
        def work(start, size):
            rows = pl.ds(pl.multiple_of(start, 8), size)
            targets = [spread[c * bins + t, rows, :] for c in range(3)]

            sums = (jnp.zeros((size, LANES), jnp.float32),) * 3
            for done, count, rounds in runs:
                sums = lax.fori_loop(
                    0, rounds, lambda i, sums, d=done, n=count: add_pairs(
                        sources, d + i * n, n, t, bins, targets, sums
                    ), sums
                )
            for c in range(3):
                totals[c * bins + t, rows, :] = sums[c]

        live = (all_counts[1, t, 0, z] + 7) // 8 * 8
        first = jnp.int32(0)
        for size in GROUPS:
            groups = (live - first) // size

            def one_group(group, carry, first=first, size=size):
                work(first + group * size, size)
                return carry

            lax.fori_loop(0, groups, one_group, 0)
            first = first + groups * size
        return carry

    lax.fori_loop(0, bins, one_bin, 0)

    for half in range(halves):
        lanes = slice(half * LANES, (half + 1) * LANES)
        columns[...] = jnp.zeros_like(columns)
        for t in range(bins):

            @pl.when(all_counts[1, t, 0, z] > half * LANES)
            def _():
                found = columns[...]
                for c in range(3):
                    at = c * bins + t
                    found = jnp.where(
                        wide_lane == at, jnp.sum(totals[at, lanes, :], axis=1, keepdims=True), found
                    )
                columns[...] = found

        summed = jnp.transpose(columns[...])
        for t in range(bins):
            alive = lane[0:1] + half * LANES < all_counts[1, t, 0, z]
            for c in range(3):
                at = c * bins + t
                force = summed[at : at + 1] + forces[at, :, lanes]
                accel = jnp.where(alive, force * (strength / slots), 0.0)
                speed = speeds[at, :, lanes] + time_step * accel
                speeds[at, :, lanes] = speed
                places[at, :, lanes] = places[at, :, lanes] + time_step * speed
    stores = [
        pltpu.make_async_copy(places, places_out, sems.at[0]),
        pltpu.make_async_copy(speeds, speeds_out, sems.at[1]),
    ]
    for store in stores:
        store.start()
    for store in stores:
        store.wait()


def on_device(positions, velocities, masses, counts, neighbours):
    bins, slots = positions.shape[3:]
    helpers = counts.shape[1]
    sides = len(SIDES)
    hbm = pl.BlockSpec(memory_space=pltpu.HBM)
    dma = pltpu.SemaphoreType.DMA

    def floats(*shape):
        return jax.ShapeDtypeStruct(shape, jnp.float32)

    places = positions.reshape(3 * bins, 1, slots)
    speeds = velocities.reshape(3 * bins, 1, slots)
    masses = masses.reshape(bins, 1, slots)
    counts = counts.transpose(2, 0, 1)
    links = neighbours.transpose(0, 2, 1, 3)

    state = floats(3 * bins, 1, slots)
    work = [
        pltpu.VMEM(state.shape, jnp.float32),
        pltpu.VMEM(masses.shape, jnp.float32),
        pltpu.SMEM(counts.shape, jnp.int32),
        pltpu.SMEM(links.shape, jnp.int32),
        pltpu.VMEM(state.shape, jnp.float32),
        pltpu.VMEM((bins * slots // LANES, 8, LANES), jnp.float32),
        pltpu.VMEM((3 * bins, slots, LANES), jnp.float32),
        pltpu.VMEM((3 * bins, slots, LANES), jnp.float32),
        pltpu.VMEM((LANES, LANES), jnp.float32),
        dma((5,)),
    ]
    halo, mass_halo, all_counts, forces = pl.pallas_call(
        first_exchange,
        out_shape=(
            floats(sides, 3 * bins, 1, slots),
            floats(sides, bins, 1, slots),
            jax.ShapeDtypeStruct((3, bins, 1, helpers), jnp.int32),
            state,
        ),
        in_specs=[hbm] * 4,
        out_specs=(hbm,) * 4,
        scratch_shapes=[dma((sides,))] * 4 + [dma((3,))] * 2 + work,
        compiler_params=pltpu.CompilerParams(collective_id=0, has_side_effects=True),
        name="first_exchange",
    )(places, masses, counts, links)

    exchange = pl.pallas_call(
        later_exchange,
        out_shape=(floats(sides, 3 * bins, 1, slots), state),
        in_specs=[hbm] * 4,
        out_specs=(hbm, hbm),
        scratch_shapes=[dma((sides,))] * 2 + work,
        compiler_params=pltpu.CompilerParams(collective_id=1, has_side_effects=True),
        name="later_exchange",
    )

    tiles = sides * bins * slots // LANES + slots // LANES + 1
    step = pl.pallas_call(
        step_kernel,
        out_shape=(state, state),
        in_specs=[hbm] * 7,
        out_specs=(hbm, hbm),
        scratch_shapes=[
            pltpu.SMEM((3, bins, 1, helpers), jnp.int32),
            pltpu.SMEM(links.shape, jnp.int32),
            pltpu.VMEM(halo.shape, jnp.float32),
            pltpu.VMEM(mass_halo.shape, jnp.float32),
            pltpu.VMEM(state.shape, jnp.float32),
            pltpu.VMEM(state.shape, jnp.float32),
            pltpu.VMEM(state.shape, jnp.float32),
            pltpu.VMEM((tiles, 8, LANES), jnp.float32),
            pltpu.VMEM((3 * bins, slots, LANES), jnp.float32),
            pltpu.VMEM((3 * bins, slots, LANES), jnp.float32),
            pltpu.VMEM((LANES, LANES), jnp.float32),
            dma((7,)),
        ],
        name="step",
    )
    for substep in range(SUBSTEPS):
        if substep > 0:
            halo, forces = exchange(places, masses, counts, links)
        places, speeds = step(all_counts, links, halo, mass_halo, places, forces, speeds)
    return places.reshape(positions.shape), speeds.reshape(velocities.shape)


def solution(mesh):
    return jax.shard_map(
        on_device,
        mesh=mesh,
        in_specs=(
            P(None, "dom", "help", None, None),
            P(None, "dom", "help", None, None),
            P("dom", "help", None, None),
            P("dom", None, None),
            P("dom", None, None, None),
        ),
        out_specs=(P(None, "dom", "help", None, None), P(None, "dom", "help", None, None)),
        check_vma=False,
    )
```

```python
import jax
import jax.numpy as jnp
from jax import lax
from jax.experimental import pallas as pl
from jax.experimental.pallas import tpu as pltpu
from jax.sharding import PartitionSpec as P

SUBSTEPS = 3
LANES = 128
GROUPS = (32, 16, 8)
TILES = (16, 8, 4, 2, 1)

softening = 0.25
strength = 4.0
time_step = 0.2

SIDES = [(dx, dz) for dx in (-1, 0, 1) for dz in (-1, 0, 1) if (dx, dz) != (0, 0)]


def partner(dx, dz):
    def at(axis, step):
        count = lax.axis_size(axis)
        return lax.rem(lax.axis_index(axis) + (step + count), count)

    return {"dom": at("dom", dx), "help": at("help", dz)}


def greet():
    barrier = pltpu.get_barrier_semaphore()
    for dx, dz in SIDES:
        pl.semaphore_signal(
            barrier, inc=1, device_id=partner(dx, dz), device_id_type=pl.DeviceIdType.MESH
        )
    return barrier


def column_copies(column, halo, send_sem, recv_sem):
    last = len(SIDES) - 1
    return [
        pltpu.make_async_remote_copy(
            src_ref=column,
            dst_ref=halo.at[last - index],
            send_sem=send_sem.at[index],
            recv_sem=recv_sem.at[last - index],
            device_id=partner(dx, dz),
            device_id_type=pl.DeviceIdType.MESH,
        )
        for index, (dx, dz) in enumerate(SIDES)
    ]


def lane_and_row():
    shape = (8, LANES)
    return lax.broadcasted_iota(jnp.int32, shape, 1), lax.broadcasted_iota(jnp.int32, shape, 0)


def bin_shift(links, z, dx, dz, s, bins):
    _, row = lane_and_row()
    shift = jnp.where(row == 0, float(dx), jnp.where(row == bins + 1, float(dz), 0.0))
    for t in range(bins):
        below = links[0, t, z, (dx + 1) * 9 + (dz + 1) * 3] == s
        above = links[0, t, z, (dx + 1) * 9 + (dz + 1) * 3 + 2] == s
        along = jnp.where(below, -1.0, jnp.where(above, 1.0, 0.0)).astype(jnp.float32)
        shift = jnp.where(row == 1 + t, along, shift)
    return shift


def source_block(column, weights, s, half, bins, shift, live):
    lane, row = lane_and_row()
    lanes = slice(half * LANES, (half + 1) * LANES)
    line = [
        jnp.broadcast_to(part, (8, LANES))
        for part in [column[c * bins + s, :, lanes] for c in range(3)] + [weights[s, :, lanes]]
    ]
    block = jnp.where(row == bins + 1, line[2], line[3])
    block = jnp.where(row <= bins, line[1], block)
    block = jnp.where(row == 0, line[0], block)
    return jnp.where(lane + half * LANES < live, block + shift, 0.0)


def spread_targets(places, columns, spread):
    columns[...] = jnp.zeros_like(columns)
    rows, slots = spread.shape[:2]
    for half in range(slots // LANES):
        lanes = slice(half * LANES, (half + 1) * LANES)
        for i in range(rows):
            columns[i : i + 1, :] = places[i, :, lanes]
        turned = jnp.transpose(columns[...])
        for i in range(rows):
            spread[i, lanes, :] = jnp.broadcast_to(turned[:, i : i + 1], (LANES, LANES))


def add_pairs(sources, first, count, t, bins, targets, sums):
    sums = list(sums)
    for k in range(count):
        tile = first + k
        sx = sources[tile, 0:1, :]
        sy = sources[tile, pl.ds(1 + t, 1), :]
        sz = sources[tile, bins + 1 : bins + 2, :]
        mass = sources[tile, bins + 2 : bins + 3, :]
        ex = sx - targets[0]
        ey = sy - targets[1]
        ez = sz - targets[2]
        inverse = lax.rsqrt(ex * ex + ey * ey + (ez * ez + softening))
        weight = (mass * inverse) * (inverse * inverse)
        sums[0] = sums[0] + weight * ex
        sums[1] = sums[1] + weight * ey
        sums[2] = sums[2] + weight * ez
    return tuple(sums)


def own_column(places, masses, counts, links, forces, sources, spread, totals, columns):
    bins, _, slots = masses.shape
    halves = slots // LANES
    z = lax.axis_index("help")
    for s in range(bins):
        shift = bin_shift(links, z, 0, 0, s, bins)
        for half in range(halves):
            sources[s * halves + half] = source_block(
                places, masses, s, half, bins, shift, counts[s, 0, z]
            )
    spread_targets(places, columns, spread)
    groups = slots // GROUPS[0]

    def work(group, carry):
        t = group // groups
        rows = pl.ds(pl.multiple_of(group % groups * GROUPS[0], GROUPS[0]), GROUPS[0])
        targets = [spread[c * bins + t, rows, :] for c in range(3)]
        zero = jnp.zeros((GROUPS[0], LANES), jnp.float32)
        sums = add_pairs(sources, 0, bins * halves, t, bins, targets, (zero, zero, zero))
        for c in range(3):
            totals[c * bins + t, rows, :] = sums[c]
        return carry

    lax.fori_loop(0, bins * groups, work, 0)
    wide_lane = lax.broadcasted_iota(jnp.int32, (LANES, LANES), 1)
    for half in range(halves):
        lanes = slice(half * LANES, (half + 1) * LANES)
        found = jnp.zeros((LANES, LANES), jnp.float32)
        for at in range(3 * bins):
            found = jnp.where(
                wide_lane == at, jnp.sum(totals[at, lanes, :], axis=1, keepdims=True), found
            )
        summed = jnp.transpose(found)
        for at in range(3 * bins):
            forces[at, :, lanes] = summed[at : at + 1]


def exchange_beside_work(copies, inputs, forces_out, local, work, sems):
    fetches = [
        pltpu.make_async_copy(there, here, sems.at[i])
        for i, (there, here) in enumerate(zip(inputs, local[:4]))
    ]
    barrier = greet()
    for fetch in fetches:
        fetch.start()
    pl.semaphore_wait(barrier, len(SIDES))
    for copy in copies:
        copy.start()
    for fetch in fetches:
        fetch.wait()
    own_column(*local, *work)
    store = pltpu.make_async_copy(local[4], forces_out, sems.at[4])
    store.start()
    for copy in copies:
        copy.wait()
    store.wait()


def first_exchange(places, masses, counts, links, halo, mass_halo, all_counts, forces, *rest):
    sems, local, work, fetch_sems = rest[:6], rest[6:11], rest[11:15], rest[15]
    copies = column_copies(places, halo, sems[0], sems[1])
    copies += column_copies(masses, mass_halo, sems[2], sems[3])
    for dx in (-1, 1):
        copies.append(
            pltpu.make_async_remote_copy(
                src_ref=counts,
                dst_ref=all_counts.at[1 - dx],
                send_sem=sems[4].at[1 + dx],
                recv_sem=sems[5].at[1 - dx],
                device_id=partner(dx, 0),
                device_id_type=pl.DeviceIdType.MESH,
            )
        )
    copies.append(pltpu.make_async_copy(counts, all_counts.at[1], sems[4].at[1]))
    exchange_beside_work(copies, (places, masses, counts, links), forces, local, work, fetch_sems)


def later_exchange(places, masses, counts, links, halo, forces, *rest):
    sems, local, work, fetch_sems = rest[:2], rest[2:7], rest[7:11], rest[11]
    copies = column_copies(places, halo, sems[0], sems[1])
    exchange_beside_work(copies, (places, masses, counts, links), forces, local, work, fetch_sems)


def step_kernel(
    counts_in, links_in, halo_in, mass_halo_in, places_in, forces_in, speeds_in,
    places_out, speeds_out, all_counts, links, halo, mass_halo, places, forces, speeds,
    sources, spread, totals, columns, sems,
):
    pairs = [
        (halo_in, halo),
        (mass_halo_in, mass_halo),
        (counts_in, all_counts),
        (links_in, links),
        (places_in, places),
        (forces_in, forces),
        (speeds_in, speeds),
    ]
    fetches = [
        pltpu.make_async_copy(there, here, sems.at[i]) for i, (there, here) in enumerate(pairs)
    ]
    for fetch in fetches:
        fetch.start()
    bins = mass_halo.shape[1]
    helpers = all_counts.shape[3]
    slots = mass_halo.shape[3]
    halves = slots // LANES
    z = lax.axis_index("help")
    lane, _ = lane_and_row()
    wide_lane = lax.broadcasted_iota(jnp.int32, (LANES, LANES), 1)

    for fetch in fetches:
        fetch.wait()
    spread_targets(places, columns, spread)

    sources[0] = jnp.zeros((8, LANES), jnp.float32)
    filled = jnp.int32(0)
    for index, (dx, dz) in enumerate(SIDES):
        column_z = lax.rem(z + (dz + helpers), helpers)
        for s in range(bins):
            live = all_counts[1 + dx, s, 0, column_z]
            shift = bin_shift(links, z, dx, dz, s, bins)
            tile = filled // LANES
            turn = lax.rem(filled, LANES)
            kept = lane >= turn
            carried = sources[tile]
            for half in range(halves):
                block = source_block(
                    halo.at[index], mass_halo.at[index], s, half, bins, shift, live
                )
                turned = pltpu.roll(block, turn, 1)
                sources[tile + half] = carried + jnp.where(kept, turned, 0.0)
                carried = jnp.where(kept, 0.0, turned)
            sources[tile + halves] = carried
            filled = filled + live
    used = (filled + LANES - 1) // LANES
    runs = []
    done = jnp.int32(0)
    for count in TILES:
        rounds = (used - done) // count
        runs.append((done, count, rounds))
        done = done + rounds * count

    def one_bin(t, carry):
        def work(start, size):
            rows = pl.ds(pl.multiple_of(start, 8), size)
            targets = [spread[c * bins + t, rows, :] for c in range(3)]

            sums = (jnp.zeros((size, LANES), jnp.float32),) * 3
            for done, count, rounds in runs:
                sums = lax.fori_loop(
                    0, rounds, lambda i, sums, d=done, n=count: add_pairs(
                        sources, d + i * n, n, t, bins, targets, sums
                    ), sums
                )
            for c in range(3):
                totals[c * bins + t, rows, :] = sums[c]

        live = (all_counts[1, t, 0, z] + 7) // 8 * 8
        first = jnp.int32(0)
        for size in GROUPS:
            groups = (live - first) // size

            def one_group(group, carry, first=first, size=size):
                work(first + group * size, size)
                return carry

            lax.fori_loop(0, groups, one_group, 0)
            first = first + groups * size
        return carry

    lax.fori_loop(0, bins, one_bin, 0)

    for half in range(halves):
        lanes = slice(half * LANES, (half + 1) * LANES)
        columns[...] = jnp.zeros_like(columns)
        for t in range(bins):

            @pl.when(all_counts[1, t, 0, z] > half * LANES)
            def _():
                found = columns[...]
                for c in range(3):
                    at = c * bins + t
                    found = jnp.where(
                        wide_lane == at, jnp.sum(totals[at, lanes, :], axis=1, keepdims=True), found
                    )
                columns[...] = found

        summed = jnp.transpose(columns[...])
        for t in range(bins):
            alive = lane[0:1] + half * LANES < all_counts[1, t, 0, z]
            for c in range(3):
                at = c * bins + t
                force = summed[at : at + 1] + forces[at, :, lanes]
                accel = jnp.where(alive, force * (strength / slots), 0.0)
                speed = speeds[at, :, lanes] + time_step * accel
                speeds[at, :, lanes] = speed
                places[at, :, lanes] = places[at, :, lanes] + time_step * speed
    stores = [
        pltpu.make_async_copy(places, places_out, sems.at[0]),
        pltpu.make_async_copy(speeds, speeds_out, sems.at[1]),
    ]
    for store in stores:
        store.start()
    for store in stores:
        store.wait()


def on_device(positions, velocities, masses, counts, neighbours):
    bins, slots = positions.shape[3:]
    helpers = counts.shape[1]
    sides = len(SIDES)
    hbm = pl.BlockSpec(memory_space=pltpu.HBM)
    dma = pltpu.SemaphoreType.DMA

    def floats(*shape):
        return jax.ShapeDtypeStruct(shape, jnp.float32)

    places = positions.reshape(3 * bins, 1, slots)
    speeds = velocities.reshape(3 * bins, 1, slots)
    masses = masses.reshape(bins, 1, slots)
    counts = counts.transpose(2, 0, 1)
    links = neighbours.transpose(0, 2, 1, 3)

    state = floats(3 * bins, 1, slots)
    work = [
        pltpu.VMEM(state.shape, jnp.float32),
        pltpu.VMEM(masses.shape, jnp.float32),
        pltpu.SMEM(counts.shape, jnp.int32),
        pltpu.SMEM(links.shape, jnp.int32),
        pltpu.VMEM(state.shape, jnp.float32),
        pltpu.VMEM((bins * slots // LANES, 8, LANES), jnp.float32),
        pltpu.VMEM((3 * bins, slots, LANES), jnp.float32),
        pltpu.VMEM((3 * bins, slots, LANES), jnp.float32),
        pltpu.VMEM((LANES, LANES), jnp.float32),
        dma((5,)),
    ]
    halo, mass_halo, all_counts, forces = pl.pallas_call(
        first_exchange,
        out_shape=(
            floats(sides, 3 * bins, 1, slots),
            floats(sides, bins, 1, slots),
            jax.ShapeDtypeStruct((3, bins, 1, helpers), jnp.int32),
            state,
        ),
        in_specs=[hbm] * 4,
        out_specs=(hbm,) * 4,
        scratch_shapes=[dma((sides,))] * 4 + [dma((3,))] * 2 + work,
        compiler_params=pltpu.CompilerParams(collective_id=0, has_side_effects=True),
        name="first_exchange",
    )(places, masses, counts, links)

    exchange = pl.pallas_call(
        later_exchange,
        out_shape=(floats(sides, 3 * bins, 1, slots), state),
        in_specs=[hbm] * 4,
        out_specs=(hbm, hbm),
        scratch_shapes=[dma((sides,))] * 2 + work,
        compiler_params=pltpu.CompilerParams(collective_id=1, has_side_effects=True),
        name="later_exchange",
    )

    tiles = sides * bins * slots // LANES + slots // LANES + 1
    step = pl.pallas_call(
        step_kernel,
        out_shape=(state, state),
        in_specs=[hbm] * 7,
        out_specs=(hbm, hbm),
        scratch_shapes=[
            pltpu.SMEM((3, bins, 1, helpers), jnp.int32),
            pltpu.SMEM(links.shape, jnp.int32),
            pltpu.VMEM(halo.shape, jnp.float32),
            pltpu.VMEM(mass_halo.shape, jnp.float32),
            pltpu.VMEM(state.shape, jnp.float32),
            pltpu.VMEM(state.shape, jnp.float32),
            pltpu.VMEM(state.shape, jnp.float32),
            pltpu.VMEM((tiles, 8, LANES), jnp.float32),
            pltpu.VMEM((3 * bins, slots, LANES), jnp.float32),
            pltpu.VMEM((3 * bins, slots, LANES), jnp.float32),
            pltpu.VMEM((LANES, LANES), jnp.float32),
            dma((7,)),
        ],
        name="step",
    )
    for substep in range(SUBSTEPS):
        if substep > 0:
            halo, forces = exchange(places, masses, counts, links)
        places, speeds = step(all_counts, links, halo, mass_halo, places, forces, speeds)
    return places.reshape(positions.shape), speeds.reshape(velocities.shape)


def solution(mesh):
    return jax.shard_map(
        on_device,
        mesh=mesh,
        in_specs=(
            P(None, "dom", "help", None, None),
            P(None, "dom", "help", None, None),
            P("dom", "help", None, None),
            P("dom", None, None),
            P("dom", None, None, None),
        ),
        out_specs=(P(None, "dom", "help", None, None), P(None, "dom", "help", None, None)),
        check_vma=False,
    )
```
